1024 devices in a mesh: row: 8 (over z_hi, core), col: 128 (over z_lo, y, x).
Axes of the slice: x: 4, y: 8, z: 16 (z_hi: 4, z_lo: 4; z = z_hi * 4 + z_lo), core: 2. Of those that a mesh axis runs over, the one named last changes fastest.
Arguments:
- user_emb: bfloat16 [32768, 64], P(('row', 'col')), may hold values from -6 to 6
- item_emb: bfloat16 [65536, 64], P(('row', 'col')), may hold values from -6 to 6
- user_degree: int32 [32768], P(('row', 'col')), may hold values from 1 to 16
- item_degree: int32 [65536], P(('row', 'col')), may hold values from 1 to 16
- block_values: bfloat16 [8, 128, 8, 128, 128], P('row', 'col'), may hold values from 0 to 1, as said below
- block_row: int32 [8, 128, 8], P('row', 'col'), may hold values from 0 to 31, as said below
- block_col: int32 [8, 128, 8], P('row', 'col'), may hold values from 0 to 3, as said below
- block_count: int32 [8, 128], P('row', 'col'), may hold values from 1 to 8, as said below
Outputs:
- user_final: bfloat16 [32768, 64], P(('row', 'col'))
- item_final: bfloat16 [65536, 64], P(('row', 'col'))
The draws below stay inside these ranges and needn't reach their ends.
Inputs may be any that keep to these rules, and one draw needn't show every extreme that they name: `block_row`: slot tile rows within one user group; the live slots of a device name distinct tiles. `block_col`: slot tile columns within one item shard. `block_count`: slots at or beyond the count are ignored; some device has all 8 slots live. `block_values`: nonnegative weights; most entries of a tile are zero.
All inputs are finite; a program needn't handle non-finite values.
Results may differ from the reference program's by a relative error of at most 0.0045.
Values may be sent and summed in bfloat16 or wider, within the bound.
No kernel may reach another device: no remote copies, remote signals or barrier semaphores. Data moves between devices by JAX's collectives and lax.ppermute only.
A program may use at most 32 MiB of HBM per device.

```python
import math
import jax
import jax.numpy as jnp
from jax import lax

EMB = 64
BS = 128
LAYERS = 2
UB = 32
IB = 4
NBLK = 8
GROUP = 4096
SHARD = 512
I_DEV = 64
USERS = 32768
ITEMS = 65536
N_ROW = 8
N_COL = 128


def cell_order(key):
    device_keys = jax.random.split(key, N_ROW * N_COL)

    def shuffle_one(device_key):
        return jax.random.permutation(device_key, UB * IB)[:NBLK]
    shuffled = jax.vmap(shuffle_one)(device_keys)
    return shuffled.reshape(N_ROW, N_COL, NBLK).astype(jnp.int32)


def draw_block_row(key, part):
    return (cell_order(key) // IB).astype(jnp.int32)


def draw_block_col(key, part):
    return (cell_order(key) % IB).astype(jnp.int32)


def draw_block_count(key, part):
    key = jax.random.fold_in(key, 11)
    first_key, second_key = jax.random.split(key)
    levels = jax.random.randint(first_key, (N_ROW * N_COL,), 0, 4)
    counts = jnp.maximum(NBLK // jnp.left_shift(jnp.ones_like(levels), levels), 1)
    chosen = jax.random.randint(second_key, (), 0, N_ROW * N_COL)
    counts = counts.at[chosen].set(NBLK)
    return counts.reshape(N_ROW, N_COL).astype(jnp.int32)


def draw_block_values(key, part):
    key = jax.random.fold_in(key, 17)
    first_key, second_key = jax.random.split(key)
    full_shape = (N_ROW, N_COL, NBLK, BS, BS)
    keep_entry = jax.random.uniform(first_key, full_shape, jnp.float32) < 0.0625
    weight = jnp.exp(jax.random.uniform(second_key, full_shape, jnp.float32, math.log(0.1), 0.0))
    return jnp.where(keep_entry, weight, 0.0).astype(jnp.bfloat16)


def with_ends(result, stream_key, smallest, high):
    shape = result.shape
    index_at = [jax.random.randint(jax.random.fold_in(stream_key, axis), (), 0, shape[axis]) for axis in range(len(shape))]
    result = result.at[tuple(index_at)].set(smallest)
    longest = shape.index(max(shape))
    index_at[longest] = (index_at[longest] + 1) % shape[longest]
    return result.at[tuple(index_at)].set(high)


def level_of(rng, shape, pieces, low, top_value):
    factor_of, own = 1.0, jax.random.fold_in(rng, 6)
    for axis_at, shards_of in pieces:
        heights = jnp.exp(jax.random.uniform(jax.random.fold_in(own, axis_at), (shards_of,), jnp.float32, low / len(pieces), top_value / len(pieces)))
        factor_of = factor_of * jnp.repeat(heights, shape[axis_at] // shards_of).reshape([-1 if axis == axis_at else 1 for axis in range(len(shape))])
    return factor_of


def bell_draw(stream_key, dims, scale, most, cuts=(), kind=jnp.bfloat16):
    drawn = scale * jax.random.normal(stream_key, dims, jnp.float32)
    if cuts:
        drawn = drawn * level_of(stream_key, dims, cuts, -0.22, 0.18)
    return jnp.clip(drawn, -most, most).astype(kind)


def setup_inputs(seed: int = 0) -> dict:
    key_of = jax.random.split(jax.random.key(seed), 9)
    user_emb = bell_draw(key_of[0], (USERS, EMB), 1.0, 6.0, ((0, 1024),))
    item_emb = bell_draw(key_of[1], (ITEMS, EMB), 1.0, 6.0, ((0, 1024),))
    user_degree = with_ends(jax.random.randint(key_of[2], (USERS,), 1, 17), jax.random.fold_in(key_of[2], 1), 1, 16).astype(jnp.int32)
    item_degree = with_ends(jax.random.randint(key_of[3], (ITEMS,), 1, 17), jax.random.fold_in(key_of[3], 1), 1, 16).astype(jnp.int32)
    block_values = draw_block_values(jax.random.fold_in(key_of[8], 71), 0)
    block_row = draw_block_row(jax.random.fold_in(key_of[8], 71), 0)
    block_col = draw_block_col(jax.random.fold_in(key_of[8], 71), 0)
    block_count = draw_block_count(jax.random.fold_in(key_of[8], 71), 0)
    return {"user_emb": user_emb, "item_emb": item_emb, "user_degree": user_degree, "item_degree": item_degree, "block_values": block_values, "block_row": block_row, "block_col": block_col, "block_count": block_count}


def slot_terms(tile_values, slot_rows, slot_cols, count, item_block, user_block):
    num_rows = user_block.shape[0] // BS
    num_cols = item_block.shape[0] // BS
    live_slots = jnp.arange(NBLK, dtype=jnp.int32) < count
    row_pick = ((slot_rows[:, None] == jnp.arange(num_rows, dtype=jnp.int32)[None, :]) & live_slots[:, None]).astype(jnp.float32)
    col_pick = ((slot_cols[:, None] == jnp.arange(num_cols, dtype=jnp.int32)[None, :]) & live_slots[:, None]).astype(jnp.float32)
    values = tile_values.astype(jnp.float32)
    hp = lax.Precision.HIGHEST
    item_pick = jnp.einsum('bc,cte->bte', col_pick, item_block.astype(jnp.float32).reshape(num_cols, BS, EMB), precision=hp)
    user_pick = jnp.einsum('bu,use->bse', row_pick, user_block.astype(jnp.float32).reshape(num_rows, BS, EMB), precision=hp)
    user_part = jnp.einsum('bu,bse->use', row_pick, jnp.einsum('bst,bte->bse', values, item_pick, precision=hp), precision=hp)
    item_part = jnp.einsum('bc,bte->cte', col_pick, jnp.einsum('bst,bse->bte', values, user_pick, precision=hp), precision=hp)
    return (user_part.reshape(GROUP, EMB), item_part.reshape(SHARD, EMB))

def reference(user_emb, item_emb, user_degree, item_degree, block_values, block_row, block_col, block_count):
    user_scale = lax.rsqrt(user_degree.astype(jnp.float32))[:, None]
    item_scale = lax.rsqrt(item_degree.astype(jnp.float32))[:, None]
    users_now = user_emb.astype(jnp.float32)
    items_now = item_emb.astype(jnp.float32)
    user_total = users_now
    item_total = items_now
    for layer_index in range(LAYERS):
        sent_users = (user_scale * users_now).astype(jnp.bfloat16)
        sent_items = (item_scale * items_now).astype(jnp.bfloat16)
        user_groups = sent_users.reshape(N_ROW, GROUP, EMB)
        item_shards = sent_items.reshape(N_ROW, N_COL, I_DEV, EMB).transpose(1, 0, 2, 3).reshape(N_COL, SHARD, EMB)

        def device_step(running, device_index):
            user_accum, item_accum = running
            group_row = device_index // N_COL
            shard_col = device_index % N_COL
            user_part, item_part = slot_terms(block_values[group_row, shard_col], block_row[group_row, shard_col], block_col[group_row, shard_col], block_count[group_row, shard_col], item_shards[shard_col], user_groups[group_row])
            user_accum = user_accum.at[group_row].add(user_part)
            item_accum = item_accum.at[shard_col].add(item_part)
            return ((user_accum, item_accum), None)
        start_state = (jnp.zeros((N_ROW, GROUP, EMB), jnp.float32), jnp.zeros((N_COL, SHARD, EMB), jnp.float32))
        (user_accum, item_accum), _ = lax.scan(device_step, start_state, jnp.arange(N_ROW * N_COL, dtype=jnp.int32))
        users_now = user_scale * user_accum.reshape(USERS, EMB)
        items_now = item_scale * item_accum.reshape(N_COL, N_ROW, I_DEV, EMB).transpose(1, 0, 2, 3).reshape(ITEMS, EMB)
        user_total = user_total + users_now
        item_total = item_total + items_now
    return ((user_total / (LAYERS + 1.0)).astype(jnp.bfloat16), (item_total / (LAYERS + 1.0)).astype(jnp.bfloat16))
```

```python
import jax
import jax.numpy as jnp
from jax import lax
from jax.experimental import pallas as pl
from jax.experimental.pallas import tpu as pltpu
from jax.sharding import PartitionSpec as P

EMB = 64
BS = 128
NBLK = 8
F32 = jnp.float32
BF16 = jnp.bfloat16

VMEM = pl.BlockSpec(memory_space=pltpu.VMEM)
SMEM = pl.BlockSpec(memory_space=pltpu.SMEM)
PARAMS = pltpu.CompilerParams(vmem_limit_bytes=24 * 1024 * 1024)


def pack_users(prod):
    parts = []
    for block in range(4):
        base = block * 32
        parts.append(
            jnp.concatenate([prod[base : base + 16, :], prod[base + 16 : base + 32, :]], axis=1)
        )
    return jnp.concatenate(parts, axis=0)


def user_products(rows, cols, count, tiles, items, lane, acc, out):
    out[...] = jnp.zeros_like(out)
    for slot in range(NBLK):
        acc[rows[0, 0, slot]] = jnp.zeros((EMB, BS), F32)
    live_slots = count[0, 0]
    for slot in range(NBLK):
        start = pl.multiple_of(cols[0, 0, slot] * BS, BS)
        prod = jnp.dot(
            tiles[0, 0, slot], items[pl.ds(start, BS), :], preferred_element_type=F32
        )
        packed = pack_users(prod[:, lane : lane + EMB])
        packed = jnp.where(slot < live_slots, packed, 0.0)
        acc[rows[0, 0, slot]] += packed
    for slot in range(NBLK):
        out[rows[0, 0, slot]] = acc[rows[0, 0, slot]].astype(BF16)


def first_users_kernel(rows, cols, count, tiles, items, out, acc):
    user_products(rows, cols, count, tiles, items, 0, acc, out)


def items_kernel(rows, cols, count, tiles, users, out, acc):
    acc[...] = jnp.zeros_like(acc)
    live_slots = count[0, 0]
    for slot in range(NBLK):
        start = pl.multiple_of(rows[0, 0, slot] * BS, BS)
        prod = lax.dot_general(
            tiles[0, 0, slot],
            users[pl.ds(start, BS), :],
            (((0,), (0,)), ((), ())),
            preferred_element_type=F32,
        )
        acc[cols[0, 0, slot]] += jnp.where(slot < live_slots, prod, 0.0)
    out[...] = acc[...].astype(BF16)


def second_users_kernel(
    mine, rows, cols, count, tiles, parts, first, item_emb, out, item_final, acc, sums, sent
):
    total = parts[0].astype(F32)
    for part in range(1, parts.shape[0]):
        total = total + parts[part].astype(F32)
    sums[...] = total
    lanes = lax.broadcasted_iota(jnp.int32, total.shape, 1)
    scale = lax.rsqrt(jnp.where(lanes >= EMB, first[...].astype(F32), 1.0))
    sent[...] = (scale * (scale * total)).astype(BF16)
    own = pl.ds(pl.multiple_of(mine[0] * EMB, EMB), EMB)
    own_scale = lax.rsqrt(first[own, :][:, EMB:].astype(F32))
    own_total = sums[own, :]
    layers = item_emb[...].astype(F32) + own_scale * own_total[:, EMB:]
    layers = layers + own_scale * own_total[:, :EMB]
    item_final[...] = (layers / 3.0).astype(BF16)
    user_products(rows, cols, count, tiles, sent, EMB, acc, out)


def unpack_sum(parts):
    total = jnp.sum(parts[...].astype(F32), axis=0)
    return jnp.concatenate([total[:, :EMB], total[:, EMB:]], axis=0)


def users_between_kernel(parts, scale, sent_first, message, users_one):
    users_now = scale[...] * unpack_sum(parts)
    users_one[...] = users_now
    sent = (scale[...] * users_now).astype(BF16)
    block = jnp.concatenate([sent, sent_first[...]], axis=1)
    message[...] = jnp.broadcast_to(block[None], message.shape)


def users_last_kernel(parts, scale, user_emb, users_one, user_final):
    layers = user_emb[...].astype(F32) + users_one[...]
    layers = layers + scale[...] * unpack_sum(parts)
    user_final[...] = (layers / 3.0).astype(BF16)


def per_device(
    user_emb, item_emb, user_degree, item_degree, block_values, block_row, block_col, block_count
):
    n_row = lax.axis_size("row")
    n_col = lax.axis_size("col")
    u_dev = user_emb.shape[0]
    i_dev = item_emb.shape[0]
    group = u_dev * n_col
    shard = i_dev * n_row
    slots = [SMEM, SMEM, SMEM, VMEM]
    slot_args = (block_row, block_col, block_count, block_values)
    user_scale = lax.rsqrt(user_degree.astype(F32))[:, None]
    item_scale = lax.rsqrt(item_degree.astype(F32))[:, None]
    sent_items = (item_scale * item_emb.astype(F32)).astype(BF16)
    sent_users = (user_scale * user_emb.astype(F32)).astype(BF16)
    user_scale = jnp.broadcast_to(user_scale, (u_dev, EMB))
    degrees = jnp.broadcast_to(item_degree.astype(BF16)[:, None], (i_dev, EMB))

    with jax.named_scope("items_0"):
        first = lax.all_gather(
            jnp.concatenate([sent_items, degrees], axis=1), "row", axis=0, tiled=True
        )
    tile_rows = group // BS
    packed_shape = jax.ShapeDtypeStruct((tile_rows, BS // 2, BS), BF16)
    acc_users = pltpu.VMEM((tile_rows, BS // 2, BS), F32)
    parts = pl.pallas_call(
        first_users_kernel,
        out_shape=packed_shape,
        in_specs=slots + [VMEM],
        out_specs=VMEM,
        scratch_shapes=[acc_users],
        compiler_params=PARAMS,
        name="users_1_parts",
    )(*slot_args, first)
    with jax.named_scope("users_1"):
        parts = lax.all_to_all(
            parts.reshape(n_col, u_dev // 2, BS), "col", split_axis=0, concat_axis=0, tiled=True
        )
    message, users_one = pl.pallas_call(
        users_between_kernel,
        out_shape=(
            jax.ShapeDtypeStruct((n_col, u_dev, BS), BF16),
            jax.ShapeDtypeStruct((u_dev, EMB), F32),
        ),
        in_specs=[VMEM] * 3,
        out_specs=(VMEM, VMEM),
        compiler_params=PARAMS,
        name="users_1_sum",
    )(parts, user_scale, sent_users)
    with jax.named_scope("sent_users"):
        users = lax.all_to_all(message, "col", split_axis=0, concat_axis=0, tiled=True)
    item_parts = pl.pallas_call(
        items_kernel,
        out_shape=jax.ShapeDtypeStruct((shard // BS, BS, BS), BF16),
        in_specs=slots + [VMEM],
        out_specs=VMEM,
        scratch_shapes=[pltpu.VMEM((shard // BS, BS, BS), F32)],
        compiler_params=PARAMS,
        name="items_parts",
    )(*slot_args, users.reshape(group, BS))
    with jax.named_scope("items_1_and_2"):
        item_parts = lax.all_gather(item_parts.reshape(shard, BS), "row", axis=0)
    mine = lax.axis_index("row").astype(jnp.int32).reshape(1)
    parts, item_final = pl.pallas_call(
        second_users_kernel,
        out_shape=(packed_shape, jax.ShapeDtypeStruct((i_dev, EMB), BF16)),
        in_specs=[SMEM] + slots + [VMEM] * 3,
        out_specs=(VMEM, VMEM),
        scratch_shapes=[
            acc_users,
            pltpu.VMEM((shard, BS), F32),
            pltpu.VMEM((shard, BS), BF16),
        ],
        compiler_params=PARAMS,
        name="users_2_parts",
    )(mine, *slot_args, item_parts, first, item_emb)
    with jax.named_scope("users_2"):
        parts = lax.all_to_all(
            parts.reshape(n_col, u_dev // 2, BS), "col", split_axis=0, concat_axis=0, tiled=True
        )
    user_final = pl.pallas_call(
        users_last_kernel,
        out_shape=jax.ShapeDtypeStruct((u_dev, EMB), BF16),
        in_specs=[VMEM] * 4,
        out_specs=VMEM,
        compiler_params=PARAMS,
        name="users_final",
    )(parts, user_scale, user_emb, users_one)
    return user_final, item_final


def solution(mesh):
    in_specs = (
        P(("row", "col"), None),
        P(("row", "col"), None),
        P(("row", "col")),
        P(("row", "col")),
        P("row", "col", None, None, None),
        P("row", "col", None),
        P("row", "col", None),
        P("row", "col"),
    )
    out_specs = (P(("row", "col"), None), P(("row", "col"), None))
    return jax.shard_map(
        per_device, mesh=mesh, in_specs=in_specs, out_specs=out_specs, check_vma=False
    )
```

```python
import jax
import jax.numpy as jnp
from jax import lax
from jax.experimental import pallas as pl
from jax.experimental.pallas import tpu as pltpu
from jax.sharding import PartitionSpec as P

EMB = 64
BS = 128
NBLK = 8
U_BLOCKS = 4
F32 = jnp.float32
BF16 = jnp.bfloat16

VMEM = pl.BlockSpec(memory_space=pltpu.VMEM)
SMEM = pl.BlockSpec(memory_space=pltpu.SMEM)
PARAMS = pltpu.CompilerParams(vmem_limit_bytes=24 * 1024 * 1024)


def fold(rows):
    half = rows.shape[0] // 2
    return jnp.concatenate([rows[:half, :], rows[half:, :]], axis=1)


def unfold(rows):
    return jnp.concatenate([rows[:, :EMB], rows[:, EMB:]], axis=0)


def user_products(rows, cols, count, tiles, items_of, acc, store):
    for slot in range(NBLK):
        acc[rows[0, 0, slot]] = jnp.zeros(acc.shape[1:], F32)
    for slot in range(NBLK):
        prod = jnp.dot(
            tiles[0, 0, slot], items_of(cols[0, 0, slot]), preferred_element_type=F32
        )
        step = BS // U_BLOCKS
        for block in range(U_BLOCKS):
            folded = fold(prod[block * step : (block + 1) * step, :])
            folded = jnp.where(slot < count[0, 0], folded, 0.0)
            acc[rows[0, 0, slot], block] += folded
    for slot in range(NBLK):
        store(rows[0, 0, slot], acc[rows[0, 0, slot]].astype(BF16))


def item_products(rows, cols, count, tiles, users_of, acc):
    acc[...] = jnp.zeros_like(acc)
    for slot in range(NBLK):
        blocks = users_of(rows[0, 0, slot])
        users = jnp.concatenate([unfold(blocks[block]) for block in range(U_BLOCKS)], axis=0)
        prod = lax.dot_general(
            tiles[0, 0, slot], users, (((0,), (0,)), ((), ())), preferred_element_type=F32
        )
        acc[cols[0, 0, slot]] += jnp.where(slot < count[0, 0], prod, 0.0)


def block_range(tile_row):
    return pl.ds(pl.multiple_of(tile_row * U_BLOCKS, U_BLOCKS), U_BLOCKS)


def tile_range(tile_col):
    return pl.ds(pl.multiple_of(tile_col * BS, BS), BS)


def users_one_kernel(rows, cols, count, tiles, first, out, acc):
    out[...] = jnp.zeros_like(out)

    def store(tile_row, value):
        out[block_range(tile_row)] = value

    user_products(
        rows, cols, count, tiles, lambda col: first[tile_range(col), :][:, EMB:], acc, store
    )


def items_one_kernel(rows, cols, count, tiles, users, out, acc):
    item_products(rows, cols, count, tiles, lambda row: users[block_range(row)], acc)
    for col in range(acc.shape[0]):
        out[col] = fold(acc[col]).astype(BF16)


def middle_kernel(
    mine, rows, cols, count, tiles, item_parts, first, user_parts, user_scale,
    message, users_one, items_one, acc, sent, scaled,
):
    total = item_parts[0].astype(F32)
    for part in range(1, item_parts.shape[0]):
        total = total + item_parts[part].astype(F32)
    for col in range(total.shape[0]):
        here = slice(col * BS, (col + 1) * BS)
        scale = lax.rsqrt(first[here, :][:, :EMB].astype(F32))
        items_now = scale * unfold(total[col])
        scaled[here, :] = items_now
        sent[here, :] = (scale * items_now).astype(BF16)
    own = items_one.shape[0]
    items_one[...] = scaled[pl.ds(pl.multiple_of(mine[0] * own, own), own), :]

    users_now = user_scale[...] * unfold(jnp.sum(user_parts[...].astype(F32), axis=0))
    users_one[...] = users_now
    block = fold((user_scale[...] * users_now).astype(BF16))
    half = block.shape[0]
    message[:, :half, :] = jnp.broadcast_to(block[None], (message.shape[0], half, BS))
    message[:, half:, :] = jnp.zeros((message.shape[0], half, BS), BF16)

    def store(tile_row, value):
        message[block_range(tile_row), half:, :] = value

    user_products(
        rows, cols, count, tiles, lambda col: sent[tile_range(col), :], acc, store
    )


def last_kernel(
    rows, cols, count, tiles, arrived, user_scale, user_emb, users_one, out, user_final, acc
):
    half = arrived.shape[1] // 2
    layers = user_emb[...].astype(F32) + users_one[...]
    parts = arrived[:, half:, :].astype(F32)
    layers = layers + user_scale[...] * unfold(jnp.sum(parts, axis=0))
    user_final[...] = (layers / 3.0).astype(BF16)
    item_products(
        rows, cols, count, tiles, lambda row: arrived[block_range(row), :half, :], acc
    )
    own = 2 * out.shape[1]
    for part in range(out.shape[0]):
        start = part * own
        out[part] = fold(acc[start // BS, start % BS : start % BS + own, :]).astype(BF16)


def items_final_kernel(parts, first, item_emb, items_one, item_final):
    total = parts[0].astype(F32)
    for part in range(1, parts.shape[0]):
        total = total + parts[part].astype(F32)
    scale = lax.rsqrt(first[:, :EMB].astype(F32))
    layers = item_emb[...].astype(F32) + items_one[...] + scale * unfold(total)
    item_final[...] = (layers / 3.0).astype(BF16)


def per_device(
    user_emb, item_emb, user_degree, item_degree, block_values, block_row, block_col, block_count
):
    n_row = lax.axis_size("row")
    n_col = lax.axis_size("col")
    u_dev = user_emb.shape[0]
    i_dev = item_emb.shape[0]
    group = u_dev * n_col
    shard = i_dev * n_row
    tile_rows, tile_cols = group // BS, shard // BS
    slots = [SMEM, SMEM, SMEM, VMEM]
    slot_args = (block_row, block_col, block_count, block_values)
    acc_users = pltpu.VMEM((tile_rows, U_BLOCKS, u_dev // 2, BS), F32)
    acc_items = pltpu.VMEM((tile_cols, BS, EMB), F32)

    user_scale = lax.rsqrt(user_degree.astype(F32))[:, None]
    item_scale = lax.rsqrt(item_degree.astype(F32))[:, None]
    sent_items = (item_scale * item_emb.astype(F32)).astype(BF16)
    sent_users = (user_scale * user_emb.astype(F32)).astype(BF16)
    user_scale = jnp.broadcast_to(user_scale, (u_dev, EMB))
    degrees = jnp.broadcast_to(item_degree.astype(BF16)[:, None], (i_dev, EMB))
    own_first = jnp.concatenate([degrees, sent_items], axis=1)

    with jax.named_scope("users_0"):
        block = jnp.concatenate([sent_users[: u_dev // 2], sent_users[u_dev // 2 :]], axis=1)
        users = lax.all_to_all(
            jnp.broadcast_to(block[None], (n_col, *block.shape)),
            "col", split_axis=0, concat_axis=0, tiled=True,
        )
    with jax.named_scope("items_0"):
        first = lax.all_gather(own_first, "row", axis=0, tiled=True)
    user_parts = pl.pallas_call(
        users_one_kernel,
        out_shape=jax.ShapeDtypeStruct((n_col, u_dev // 2, BS), BF16),
        in_specs=slots + [VMEM],
        out_specs=VMEM,
        scratch_shapes=[acc_users],
        compiler_params=PARAMS,
        name="users_1_parts",
    )(*slot_args, first)
    item_parts = pl.pallas_call(
        items_one_kernel,
        out_shape=jax.ShapeDtypeStruct((tile_cols, BS // 2, BS), BF16),
        in_specs=slots + [VMEM],
        out_specs=VMEM,
        scratch_shapes=[acc_items],
        compiler_params=PARAMS,
        name="items_1_parts",
    )(*slot_args, users)
    with jax.named_scope("users_1"):
        user_parts = lax.all_to_all(user_parts, "col", split_axis=0, concat_axis=0, tiled=True)
    with jax.named_scope("items_1"):
        item_parts = lax.all_gather(item_parts.reshape(shard // 2, BS), "row", axis=0)
    item_parts = item_parts.reshape(n_row, tile_cols, BS // 2, BS)
    mine = lax.axis_index("row").astype(jnp.int32).reshape(1)
    message, users_one, items_one = pl.pallas_call(
        middle_kernel,
        out_shape=(
            jax.ShapeDtypeStruct((n_col, u_dev, BS), BF16),
            jax.ShapeDtypeStruct((u_dev, EMB), F32),
            jax.ShapeDtypeStruct((i_dev, EMB), F32),
        ),
        in_specs=[SMEM] + slots + [VMEM] * 4,
        out_specs=(VMEM, VMEM, VMEM),
        scratch_shapes=[
            acc_users,
            pltpu.VMEM((shard, EMB), BF16),
            pltpu.VMEM((shard, EMB), F32),
        ],
        compiler_params=PARAMS,
        name="users_2_parts",
    )(mine, *slot_args, item_parts, first, user_parts, user_scale)
    with jax.named_scope("users_1_and_2"):
        arrived = lax.all_to_all(message, "col", split_axis=0, concat_axis=0, tiled=True)
    item_parts, user_final = pl.pallas_call(
        last_kernel,
        out_shape=(
            jax.ShapeDtypeStruct((n_row, i_dev // 2, BS), BF16),
            jax.ShapeDtypeStruct((u_dev, EMB), BF16),
        ),
        in_specs=slots + [VMEM] * 4,
        out_specs=(VMEM, VMEM),
        scratch_shapes=[acc_items],
        compiler_params=PARAMS,
        name="items_2_parts",
    )(*slot_args, arrived, user_scale, user_emb, users_one)
    with jax.named_scope("items_2"):
        item_parts = lax.all_to_all(item_parts, "row", split_axis=0, concat_axis=0, tiled=True)
    item_final = pl.pallas_call(
        items_final_kernel,
        out_shape=jax.ShapeDtypeStruct((i_dev, EMB), BF16),
        in_specs=[VMEM] * 4,
        out_specs=VMEM,
        compiler_params=PARAMS,
        name="items_final",
    )(item_parts, own_first, item_emb, items_one)
    return user_final, item_final


def solution(mesh):
    in_specs = (
        P(("row", "col"), None),
        P(("row", "col"), None),
        P(("row", "col")),
        P(("row", "col")),
        P("row", "col", None, None, None),
        P("row", "col", None),
        P("row", "col", None),
        P("row", "col"),
    )
    out_specs = (P(("row", "col"), None), P(("row", "col"), None))
    return jax.shard_map(
        per_device, mesh=mesh, in_specs=in_specs, out_specs=out_specs, check_vma=False
    )
```

```python
import jax
import jax.numpy as jnp
from jax import lax
from jax.experimental import pallas as pl
from jax.experimental.pallas import tpu as pltpu
from jax.sharding import Mesh, PartitionSpec as P

BS = 128
NBLK = 8
F32 = jnp.float32
BF16 = jnp.bfloat16
ROW = ("zh", "co")
PLANE = ("zl", "y")
AXES = ROW + PLANE + ("x",)

VMEM = pl.BlockSpec(memory_space=pltpu.VMEM)
HBM = pl.BlockSpec(memory_space=pltpu.HBM)
SMEM = pl.BlockSpec(memory_space=pltpu.SMEM)


def call(kernel, name, out_shape, in_specs, scratch=(), vmem=24):
    return pl.pallas_call(
        kernel,
        out_shape=out_shape,
        in_specs=in_specs,
        out_specs=jax.tree.map(lambda _: VMEM, out_shape),
        scratch_shapes=scratch,
        compiler_params=pltpu.CompilerParams(vmem_limit_bytes=vmem * 1024 * 1024),
        name=name,
    )


def fetch(pairs, sems):
    copies = [pltpu.make_async_copy(src, dst, sems.at[i]) for i, (src, dst) in enumerate(pairs)]
    for copy in copies:
        copy.start()
    return copies


def start_kernel(
    item_emb, user_emb, item_degree, user_degree, rows, cols, count, tiles, out,
    items, users, item_deg, user_deg, slot_rows, slot_cols, live, sems,
):
    share, size = out.shape[0], tiles.shape[0]
    i_dev, emb = item_emb.shape
    u_dev = user_emb.shape[0]
    step = emb // share
    pairs = [
        (item_emb, items),
        (user_emb, users),
        (item_degree, item_deg),
        (user_degree, user_deg),
        (rows, slot_rows),
        (cols, slot_cols),
        (count, live),
    ]
    small = len(pairs)
    pairs += [(tiles, out.at[to, pl.ds(2 * step, size), :]) for to in range(share)]
    copies = fetch(pairs, sems)
    for copy in copies[:small]:
        copy.wait()
    values = jnp.concatenate(
        [
            items[...].astype(F32),
            users[...].astype(F32),
            jnp.zeros((BS - i_dev - u_dev, emb), F32),
        ],
        axis=0,
    ).T
    extra = jnp.concatenate(
        [
            item_deg[...],
            user_deg[...],
            slot_rows[0],
            slot_cols[0],
            live[...],
            jnp.zeros((1, BS - i_dev - u_dev - 2 * NBLK - 1), jnp.int32),
        ],
        axis=1,
    ).astype(F32)
    for to in range(share):
        out[to, :step, :] = values[to * step : (to + 1) * step, :].astype(BF16)
        out[to, step : 2 * step, :] = jnp.broadcast_to(extra, (step, BS)).astype(BF16)
    for copy in copies[small:]:
        copy.wait()


def users_zero_kernel(i_dev, arrived, message, user_zero, user_scale):
    share, step = arrived.shape[0], message.shape[1]
    u_dev = BS // share
    lanes = slice(i_dev, i_dev + u_dev)
    first = jnp.concatenate([arrived[x, :step, :].astype(F32)[:, lanes] for x in range(share)], 1)
    degree = jnp.concatenate([arrived[x, step : 2 * step, :].astype(F32)[:, lanes] for x in range(share)], 1)
    scale = lax.rsqrt(degree)
    user_zero[...] = first
    user_scale[...] = scale
    message[...] = jnp.broadcast_to((scale * first).astype(BF16)[None], message.shape)


def slot_list(slots, arrived):
    first = arrived.shape[1] - NBLK * BS
    for x in range(arrived.shape[0]):
        for slot in range(NBLK):
            live = slot < slots[x, 2 * NBLK]
            tile = arrived[x, first + slot * BS : first + (slot + 1) * BS, :]
            yield x, slots[x, slot], slots[x, NBLK + slot], live, tile


def item_products(slots, arrived, users, acc):
    acc[...] = jnp.zeros_like(acc)
    for x, row, col, live, tile in slot_list(slots, arrived):
        prod = jnp.dot(users[row], tile, preferred_element_type=F32)
        acc[x, col] += jnp.where(live, prod, 0.0)


def items_one_kernel(slots, arrived, users, out, acc):
    item_products(slots, arrived, users, acc)
    share, tile_cols = acc.shape[:2]
    for x in range(share):
        for col in range(tile_cols):
            out[x * tile_cols + col] = acc[x, col].astype(BF16)
    step = acc.shape[2]
    half = BS // 2
    base = share * tile_cols
    for pair in range(share // 2):
        two = [arrived[2 * pair + k, : 2 * step].astype(F32)[:, :half] for k in range(2)]
        first = jnp.concatenate([both[:step] for both in two], axis=1)
        degree = jnp.concatenate([both[step:] for both in two], axis=1)
        out[base + pair] = (lax.rsqrt(degree) * first).astype(BF16)
        out[base + share // 2 + pair] = degree.astype(BF16)


def users_kernel(slots, arrived, gathered, out, item_sum, acc, sent):
    share, tile_cols, step = item_sum.shape[:3]
    n_row = gathered.shape[0]
    half = BS // 2
    base = share * tile_cols

    def of_tile(block, x, col):
        pair, side = block + x // 2, (x % 2) * half
        return jnp.concatenate(
            [gathered[2 * col + k, pair].astype(F32)[:, side : side + half] for k in range(2)],
            axis=1,
        )

    for x in range(share):
        for col in range(tile_cols):
            at = x * tile_cols + col
            total = gathered[0, at].astype(F32)
            for part in range(1, n_row):
                total = total + gathered[part, at].astype(F32)
            item_sum[x, col] = total
            scale = lax.rsqrt(of_tile(base + share // 2, x, col))
            sent[x, col, :step] = of_tile(base, x, col).astype(BF16)
            sent[x, col, step:] = (scale * (scale * total)).astype(BF16)
    acc[...] = jnp.zeros_like(acc)
    for x, row, col, live, tile in slot_list(slots, arrived):
        prod = lax.dot_general(
            sent[x, col], tile, (((1,), (1,)), ((), ())), preferred_element_type=F32
        )
        acc[row] += jnp.where(live, prod, 0.0)
    out[...] = acc[...].astype(BF16)


def users_sum_kernel(parts, user_zero, user_scale, message, user_final):
    step = message.shape[1]
    total = parts[0].astype(F32)
    for part in range(1, parts.shape[0]):
        total = total + parts[part].astype(F32)
    scale = user_scale[...]
    users_one = scale * total[:step]
    users_two = scale * total[step:]
    message[...] = jnp.broadcast_to((scale * users_one).astype(BF16)[None], message.shape)
    user_final[...] = (user_zero[...] + users_one + users_two) / 3.0


def items_two_kernel(slots, arrived, users, item_sum, user_final, out, acc):
    item_products(slots, arrived, users, acc)
    share, tile_cols, step = acc.shape[:3]
    n_row = 2 * tile_cols
    half = BS // 2
    u_dev = BS // share
    for x in range(share):
        own = user_final[...][:, x * u_dev : (x + 1) * u_dev]
        for col in range(tile_cols):
            total = acc[x, col] + item_sum[x, col] * (1.0 / n_row)
            for k in range(2):
                block = jnp.concatenate(
                    [total[:, k * half : (k + 1) * half], own, jnp.zeros((step, half - u_dev), F32)],
                    axis=1,
                )
                out[2 * col + k, x] = block.astype(BF16)


def final_kernel(
    mine, arrived, item_emb, item_degree, item_final, user_final, items, item_deg, sems
):
    copies = fetch([(item_emb, items), (item_degree, item_deg)], sems)
    n_row, share, step = arrived.shape[:3]
    i_dev, emb = item_emb.shape
    u_dev = user_final.shape[0]
    total = arrived[0].astype(F32)
    for part in range(1, n_row):
        total = total + arrived[part].astype(F32)
    total = total.reshape(emb, BS)
    for copy in copies:
        copy.wait()
    scale = lax.rsqrt(item_deg[...].astype(F32))
    users = arrived[mine[0]].astype(F32).reshape(emb, BS)
    both = jnp.concatenate(
        [total[:, :i_dev] * scale, users[:, i_dev:]], axis=1
    ).T
    item_final[...] = ((items[...].astype(F32) + both[:i_dev]) / 3.0).astype(BF16)
    user_final[...] = both[i_dev : i_dev + u_dev].astype(BF16)


def exchange(values, axes):
    return lax.all_to_all(values, axes, split_axis=0, concat_axis=0, tiled=True)


def per_device(
    user_emb, item_emb, user_degree, item_degree, block_values, block_row, block_col, block_count
):
    share = lax.axis_size("x")
    n_row = lax.axis_size(ROW)
    tile_rows = lax.axis_size(PLANE)
    u_dev, emb = user_emb.shape
    i_dev = item_emb.shape[0]
    tile_cols = i_dev * n_row // BS
    step = emb // share
    shape = jax.ShapeDtypeStruct
    acc_items = pltpu.VMEM((share, tile_cols, step, BS), F32)

    item_degree = item_degree.reshape(1, i_dev)
    message = call(
        start_kernel,
        "start",
        shape((share, 2 * step + NBLK * BS, BS), BF16),
        [HBM] * 8,
        [
            pltpu.VMEM((i_dev, emb), BF16),
            pltpu.VMEM((u_dev, emb), BF16),
            pltpu.VMEM((1, i_dev), jnp.int32),
            pltpu.VMEM((1, u_dev), jnp.int32),
            pltpu.VMEM((1, 1, NBLK), jnp.int32),
            pltpu.VMEM((1, 1, NBLK), jnp.int32),
            pltpu.VMEM((1, 1), jnp.int32),
            pltpu.SemaphoreType.DMA((7 + share,)),
        ],
        vmem=60,
    )(
        item_emb, user_emb, item_degree, user_degree.reshape(1, u_dev),
        block_row, block_col, block_count, block_values.reshape(NBLK * BS, BS),
    )
    with jax.named_scope("base_and_tiles_along_x"):
        arrived = exchange(message, "x")
    first_slot = i_dev + u_dev
    slots = arrived[:, step, first_slot : first_slot + 2 * NBLK + 1].astype(jnp.int32)
    message, user_zero, user_scale = call(
        lambda *refs: users_zero_kernel(i_dev, *refs),
        "users_0",
        (shape((tile_rows, step, BS), BF16), shape((step, BS), F32), shape((step, BS), F32)),
        [VMEM],
    )(arrived)
    with jax.named_scope("sent_users_0"):
        users = exchange(message, PLANE)
    blocks = share * tile_cols + share
    message = call(
        items_one_kernel,
        "items_1_parts",
        shape((blocks, step, BS), BF16),
        [SMEM] + [VMEM] * 2,
        [acc_items],
    )(slots, arrived, users)
    with jax.named_scope("items_0_and_1"):
        gathered = lax.all_gather(message, ROW, axis=0)
    message, item_sum = call(
        users_kernel,
        "users_1_and_2_parts",
        (shape((tile_rows, 2 * step, BS), BF16), shape((share, tile_cols, step, BS), F32)),
        [SMEM] + [VMEM] * 2,
        [
            pltpu.VMEM((tile_rows, 2 * step, BS), F32),
            pltpu.VMEM((share, tile_cols, 2 * step, BS), BF16),
        ],
    )(slots, arrived, gathered)
    with jax.named_scope("users_1_and_2"):
        parts = exchange(message, PLANE)
    message, user_final = call(
        users_sum_kernel,
        "users_sum",
        (shape((tile_rows, step, BS), BF16), shape((step, BS), F32)),
        [VMEM] * 3,
    )(parts, user_zero, user_scale)
    with jax.named_scope("sent_users_1"):
        users = exchange(message, PLANE)
    message = call(
        items_two_kernel,
        "items_2_parts",
        shape((n_row, share, step, BS), BF16),
        [SMEM] + [VMEM] * 4,
        [acc_items],
    )(slots, arrived, users, item_sum, user_final)
    with jax.named_scope("items_2"):
        parts = exchange(message.reshape(n_row * share, step, BS), ROW + ("x",))
    mine = lax.axis_index(ROW).astype(jnp.int32).reshape(1)
    item_final, user_final = call(
        final_kernel,
        "final",
        (shape((i_dev, emb), BF16), shape((u_dev, emb), BF16)),
        [SMEM, VMEM, HBM, HBM],
        [
            pltpu.VMEM((i_dev, emb), BF16),
            pltpu.VMEM((1, i_dev), jnp.int32),
            pltpu.SemaphoreType.DMA((2,)),
        ],
    )(mine, parts.reshape(n_row, share, step, BS), item_emb, item_degree)
    return user_final, item_final


def solution(mesh):
    fine = Mesh(mesh.devices.reshape(4, 2, 4, 8, 4), AXES)
    col = PLANE + ("x",)
    in_specs = (
        P(AXES, None),
        P(AXES, None),
        P(AXES),
        P(AXES),
        P(ROW, col, None, None, None),
        P(ROW, col, None),
        P(ROW, col, None),
        P(ROW, col),
    )
    out_specs = (P(AXES, None), P(AXES, None))
    return jax.shard_map(
        per_device, mesh=fine, in_specs=in_specs, out_specs=out_specs, check_vma=False
    )
```

```python
import jax
import jax.numpy as jnp
from jax import lax
from jax.experimental import pallas as pl
from jax.experimental.pallas import tpu as pltpu
from jax.sharding import Mesh, PartitionSpec as P

BS = 128
NBLK = 8
F32 = jnp.float32
BF16 = jnp.bfloat16
ROW = ("zh", "co")
PLANE = ("zl", "y")
AXES = ROW + PLANE + ("x",)

VMEM = pl.BlockSpec(memory_space=pltpu.VMEM)
HBM = pl.BlockSpec(memory_space=pltpu.HBM)
SMEM = pl.BlockSpec(memory_space=pltpu.SMEM)


def call(kernel, name, out_shape, in_specs, scratch=(), out_specs=None, vmem=24):
    return pl.pallas_call(
        kernel,
        out_shape=out_shape,
        in_specs=in_specs,
        out_specs=out_specs or jax.tree.map(lambda _: VMEM, out_shape),
        scratch_shapes=scratch,
        compiler_params=pltpu.CompilerParams(vmem_limit_bytes=vmem * 1024 * 1024),
        name=name,
    )


def fetch(pairs, sems, first):
    copies = [
        pltpu.make_async_copy(src, dst, sems.at[first + i]) for i, (src, dst) in enumerate(pairs)
    ]
    for copy in copies:
        copy.start()
    return copies


def columns_of(values, to, step):
    half = values.shape[0] // 2
    run = step // 2
    low = values[to * run : (to + 1) * run, :]
    return jnp.concatenate([low, values[half + to * run : half + (to + 1) * run, :]], axis=0)


def start_kernel(
    item_emb, user_emb, item_degree, user_degree, rows, cols, count, tiles, payload, message,
    items, users, item_deg, user_deg, slot_rows, slot_cols, live, held, base, sems,
):
    share = message.shape[1]
    i_dev, emb = item_emb.shape
    u_dev = user_emb.shape[0]
    step = emb // share
    small = [
        (item_emb, items),
        (user_emb, users),
        (item_degree, item_deg),
        (user_degree, user_deg),
        (rows, slot_rows),
        (cols, slot_cols),
        (count, live),
    ]
    (fetched,) = fetch([(tiles, held)], sems, len(small))
    ready = fetch(small, sems, 0)
    for copy in ready:
        copy.wait()
    values = jnp.concatenate(
        [
            items[...].astype(F32),
            users[...].astype(F32),
            jnp.zeros((BS - i_dev - u_dev, emb), F32),
        ],
        axis=0,
    ).T
    extra = jnp.concatenate(
        [
            item_deg[...],
            user_deg[...],
            slot_rows[0],
            slot_cols[0],
            live[0],
            jnp.zeros((1, BS - i_dev - u_dev - 2 * NBLK - 1), jnp.int32),
        ],
        axis=1,
    ).astype(F32)
    base[share] = jnp.broadcast_to(extra, (step, BS)).astype(BF16)
    scale = lax.rsqrt(user_deg[...].astype(F32))
    for to in range(share):
        columns = columns_of(values, to, step)
        base[to] = columns.astype(BF16)
        sent = scale * columns[:, i_dev : i_dev + u_dev]
        low, high = sent[: step // 2], sent[step // 2 :]
        block = jnp.concatenate([low, low, high, high], axis=1).astype(BF16)
        message[:, to] = jnp.broadcast_to(block[None], (message.shape[0], *block.shape))
    fetched.wait()
    last = fetch(
        [
            (base, payload.at[pl.ds(0, share + 1)]),
            (held, payload.at[pl.ds(share + 1, held.shape[0])]),
        ],
        sems,
        len(small) + 1,
    )
    for copy in last:
        copy.wait()


def slot_list(place, slots, payloads):
    share = len(payloads)
    for away, payload in enumerate(payloads):
        x = lax.rem(place[1] + (share - away), share)
        step = payload.shape[1]
        blocks = BS // step
        for slot in range(NBLK):
            live = slot < slots[away, 2 * NBLK]
            first = share + 1 + slot * blocks
            tile = payload[first : first + blocks].reshape(BS, BS)
            yield x, slots[away, slot], slots[away, NBLK + slot], live, tile


def item_products(place, slots, payloads, users, acc):
    acc[...] = jnp.zeros_like(acc)
    for x, row, col, live, tile in slot_list(place, slots, payloads):
        prod = jnp.dot(users[row], tile, preferred_element_type=F32)
        acc[x, col] += jnp.where(live, prod, 0.0)


def items_one_kernel(
    place, slots, p0, p1, p2, p3, arrived, out, user_zero, user_scale, acc, users, base
):
    payloads = (p0, p1, p2, p3)
    tile_rows, share = arrived.shape[:2]
    step = users.shape[1]
    half = BS // 2
    u_dev = BS // share
    lane = lax.broadcasted_iota(jnp.int32, (step // 2, BS), 1)
    for row in range(tile_rows):
        here = jnp.zeros((step // 2, BS), F32)
        there = jnp.zeros((step // 2, BS), F32)
        for x in range(share):
            block = arrived[row, x].astype(F32)
            here = jnp.where(lane // u_dev == x, block, here)
            there = jnp.where(lane // u_dev == (x + share // 2) % share, block, there)
        there = pltpu.roll(there, half, 1)
        low = jnp.where(lane < half, here, there)
        high = jnp.where(lane < half, there, here)
        users[row] = jnp.concatenate([low, high], axis=0).astype(BF16)

    lane = lax.broadcasted_iota(jnp.int32, (step, BS), 1)
    zero = jnp.zeros((step, BS), F32)
    degree = jnp.ones((step, BS), F32)
    for away, payload in enumerate(payloads):
        x = lax.rem(place[1] + (share - away), share)
        values, extra = payload[place[1]], payload[share]
        base[x, 0], base[x, 1] = values, extra
        piece = values.astype(F32)[:, half : half + u_dev]
        zero = jnp.where(lane // u_dev == x, jnp.concatenate([piece] * share, axis=1), zero)
        piece = extra.astype(F32)[:, half : half + u_dev]
        degree = jnp.where(lane // u_dev == x, jnp.concatenate([piece] * share, axis=1), degree)
    user_zero[...] = zero
    user_scale[...] = lax.rsqrt(degree)

    item_products(place, slots, payloads, users, acc)
    tile_cols = acc.shape[1]
    for x in range(share):
        for col in range(tile_cols):
            out[x * tile_cols + col] = acc[x, col].astype(BF16)
    first_block = share * tile_cols
    for pair in range(share // 2):
        first, degree = (
            jnp.concatenate(
                [base[2 * pair + k, part].astype(F32)[:, :half] for k in range(2)], axis=1
            )
            for part in range(2)
        )
        out[first_block + pair] = (lax.rsqrt(degree) * first).astype(BF16)
        out[first_block + share // 2 + pair] = degree.astype(BF16)


def users_kernel(place, slots, p0, p1, p2, p3, gathered, out, item_sum, acc, sent):
    share, tile_cols, step = item_sum.shape[:3]
    n_row = gathered.shape[0]
    half = BS // 2
    base = share * tile_cols

    def of_tile(block, x, col):
        pair, side = block + x // 2, (x % 2) * half
        return jnp.concatenate(
            [gathered[2 * col + k, pair].astype(F32)[:, side : side + half] for k in range(2)],
            axis=1,
        )

    for x in range(share):
        for col in range(tile_cols):
            at = x * tile_cols + col
            total = gathered[0, at].astype(F32)
            for part in range(1, n_row):
                total = total + gathered[part, at].astype(F32)
            item_sum[x, col] = total
            scale = lax.rsqrt(of_tile(base + share // 2, x, col))
            sent[x, col, :step] = of_tile(base, x, col).astype(BF16)
            sent[x, col, step:] = (scale * (scale * total)).astype(BF16)
    acc[...] = jnp.zeros_like(acc)
    for x, row, col, live, tile in slot_list(place, slots, (p0, p1, p2, p3)):
        prod = lax.dot_general(
            sent[x, col], tile, (((1,), (1,)), ((), ())), preferred_element_type=F32
        )
        acc[row] += jnp.where(live, prod, 0.0)
    out[...] = acc[...].astype(BF16)


def users_sum_kernel(parts, user_zero, user_scale, message, user_final):
    step = message.shape[1]
    total = parts[0].astype(F32)
    for part in range(1, parts.shape[0]):
        total = total + parts[part].astype(F32)
    scale = user_scale[...]
    users_one = scale * total[:step]
    users_two = scale * total[step:]
    message[...] = jnp.broadcast_to((scale * users_one).astype(BF16)[None], message.shape)
    user_final[...] = (user_zero[...] + users_one + users_two) / 3.0


def items_two_kernel(
    place, slots, p0, p1, p2, p3, users, item_sum, user_final, out, acc
):
    item_products(place, slots, (p0, p1, p2, p3), users, acc)
    share, tile_cols, step = acc.shape[:3]
    n_row = 2 * tile_cols
    half = BS // 2
    u_dev = BS // share
    run, quarter = step // 2, step // 4
    for x in range(share):
        own = user_final[...][:, x * u_dev : (x + 1) * u_dev]
        own = jnp.concatenate(
            [own[p * quarter : (p + 1) * quarter, :] for p in range(4)], axis=1
        )
        for col in range(tile_cols):
            total = acc[x, col] + item_sum[x, col] * (1.0 / n_row)
            for k in range(2):
                side = total[:, k * half : (k + 1) * half]
                block = jnp.concatenate([side[:run, :], side[run:, :]], axis=1).astype(BF16)
                out[2 * col + k, x, 0] = block[:quarter, :]
                out[2 * col + k, x, 1] = block[quarter:, :]
                mine = place[0] == 2 * col + k
                out[2 * col + k, x, 2] = jnp.where(mine, own, 0.0).astype(BF16)


def final_kernel(arrived, payload, item_final, user_final):
    n_row, share = arrived.shape[:2]
    i_dev, emb = item_final.shape
    u_dev = user_final.shape[0]
    total = arrived[0].astype(F32)
    for part in range(1, n_row):
        total = total + arrived[part].astype(F32)
    run, quarter = emb // share // 2, emb // share // 4
    scale = lax.rsqrt(payload[share].astype(F32)[:1, :i_dev])
    scale = jnp.concatenate([scale, scale], axis=1)
    sums = jnp.concatenate([total[x, p] for x in range(share) for p in range(2)], axis=0)
    own = [payload[x].astype(F32)[:, :i_dev] for x in range(share)]
    own = [jnp.concatenate([one[:run], one[run:]], axis=1) for one in own]
    layers = (jnp.concatenate(own, axis=0) + scale * sums) / 3.0
    below = jnp.concatenate([total[x, 2] for x in range(share)], axis=0)
    pad = jnp.zeros((BS - sums.shape[0] - below.shape[0], BS), F32)
    both = jnp.concatenate([layers, below, pad], axis=0).T
    width = share * run
    layers = jnp.concatenate([both[:i_dev, :width], both[i_dev : 2 * i_dev, :width]], axis=1)
    item_final[...] = layers.astype(BF16)
    pieces = []
    for h in range(2):
        for x in range(share):
            for p in range(2):
                rows = slice((2 * h + p) * u_dev, (2 * h + p + 1) * u_dev)
                first = width + x * quarter
                pieces.append(both[rows, first : first + quarter])
    user_final[...] = jnp.concatenate(pieces, axis=1).astype(BF16)


def exchange(values, axes):
    return lax.all_to_all(values, axes, split_axis=0, concat_axis=0, tiled=True)


def per_device(
    user_emb, item_emb, user_degree, item_degree, block_values, block_row, block_col, block_count
):
    share = lax.axis_size("x")
    n_row = lax.axis_size(ROW)
    tile_rows = lax.axis_size(PLANE)
    n_col = tile_rows * share
    u_dev, emb = user_emb.shape
    i_dev = item_emb.shape[0]
    tile_cols = i_dev * n_row // BS
    step = emb // share
    shape = jax.ShapeDtypeStruct
    acc_items = pltpu.VMEM((share, tile_cols, step, BS), F32)

    item_degree = item_degree.reshape(1, i_dev)
    held = NBLK * BS // step
    payload, message = call(
        start_kernel,
        "start",
        (shape((share + 1 + held, step, BS), BF16), shape((tile_rows, share, step // 2, BS), BF16)),
        [HBM] * 8,
        [
            pltpu.VMEM((i_dev, emb), BF16),
            pltpu.VMEM((u_dev, emb), BF16),
            pltpu.VMEM((1, i_dev), jnp.int32),
            pltpu.VMEM((1, u_dev), jnp.int32),
            pltpu.VMEM((1, 1, NBLK), jnp.int32),
            pltpu.VMEM((1, 1, NBLK), jnp.int32),
            pltpu.VMEM((1, 1, 1), jnp.int32),
            pltpu.VMEM((held, step, BS), BF16),
            pltpu.VMEM((share + 1, step, BS), BF16),
            pltpu.SemaphoreType.DMA((10,)),
        ],
        (HBM, VMEM),
        vmem=60,
    )(
        item_emb, user_emb, item_degree, user_degree.reshape(1, u_dev), block_row, block_col,
        block_count.reshape(1, 1, 1), block_values.reshape(held, step, BS),
    )
    with jax.named_scope("sent_users_0"):
        arrived = exchange(message.reshape(n_col, step // 2, BS), PLANE + ("x",))
    with jax.named_scope("payloads_along_x"):
        payloads = [payload] + [
            lax.ppermute(payload, "x", [(x, (x + away) % share) for x in range(share)])
            for away in range(1, share)
        ]
    place = jnp.stack([lax.axis_index(ROW), lax.axis_index("x")]).astype(jnp.int32)
    first_slot = i_dev + u_dev
    slots = jnp.stack(
        [one[share, 0, first_slot : first_slot + 2 * NBLK + 1] for one in payloads]
    ).astype(jnp.int32)
    slotted = [SMEM] * 2 + [VMEM] * share
    slot_args = (place, slots, *payloads)
    blocks = share * tile_cols + share
    message, user_zero, user_scale = call(
        items_one_kernel,
        "items_1_parts",
        (shape((blocks, step, BS), BF16), shape((step, BS), F32), shape((step, BS), F32)),
        slotted + [VMEM],
        [
            acc_items,
            pltpu.VMEM((tile_rows, step, BS), BF16),
            pltpu.VMEM((share, 2, step, BS), BF16),
        ],
    )(*slot_args, arrived.reshape(tile_rows, share, step // 2, BS))
    with jax.named_scope("items_0_and_1"):
        gathered = lax.all_gather(message, ROW, axis=0)
    message, item_sum = call(
        users_kernel,
        "users_1_and_2_parts",
        (shape((tile_rows, 2 * step, BS), BF16), shape((share, tile_cols, step, BS), F32)),
        slotted + [VMEM],
        [
            pltpu.VMEM((tile_rows, 2 * step, BS), F32),
            pltpu.VMEM((share, tile_cols, 2 * step, BS), BF16),
        ],
    )(*slot_args, gathered)
    with jax.named_scope("users_1_and_2"):
        parts = exchange(message, PLANE)
    message, user_final = call(
        users_sum_kernel,
        "users_sum",
        (shape((tile_rows, step, BS), BF16), shape((step, BS), F32)),
        [VMEM] * 3,
    )(parts, user_zero, user_scale)
    with jax.named_scope("sent_users_1"):
        users = exchange(message, PLANE)
    message = call(
        items_two_kernel,
        "items_2_parts",
        shape((n_row, share, 3, step // 4, BS), BF16),
        slotted + [VMEM] * 3,
        [acc_items],
    )(*slot_args, users, item_sum, user_final)
    with jax.named_scope("items_2"):
        parts = exchange(message.reshape(n_row * share, *message.shape[2:]), ROW + ("x",))
    item_final, user_final = call(
        final_kernel,
        "final",
        (shape((i_dev, emb), BF16), shape((u_dev, emb), BF16)),
        [VMEM, VMEM],
    )(parts.reshape(message.shape), payload)
    return user_final, item_final


def solution(mesh):
    fine = Mesh(mesh.devices.reshape(4, 2, 4, 8, 4), AXES)
    col = PLANE + ("x",)
    in_specs = (
        P(AXES, None),
        P(AXES, None),
        P(AXES),
        P(AXES),
        P(ROW, col, None, None, None),
        P(ROW, col, None),
        P(ROW, col, None),
        P(ROW, col),
    )
    out_specs = (P(AXES, None), P(AXES, None))
    return jax.shard_map(
        per_device, mesh=fine, in_specs=in_specs, out_specs=out_specs, check_vma=False
    )
```

```python
import jax
import jax.numpy as jnp
from jax import lax
from jax.experimental import pallas as pl
from jax.experimental.pallas import tpu as pltpu
from jax.sharding import Mesh, PartitionSpec as P

BS = 128
NBLK = 8
F32 = jnp.float32
BF16 = jnp.bfloat16
ROW = ("zh", "co")
PLANE = ("zl", "y")
AXES = ROW + PLANE + ("x",)

VMEM = pl.BlockSpec(memory_space=pltpu.VMEM)
HBM = pl.BlockSpec(memory_space=pltpu.HBM)
SMEM = pl.BlockSpec(memory_space=pltpu.SMEM)


def call(kernel, name, out_shape, in_specs, scratch=(), out_specs=None, vmem=24):
    return pl.pallas_call(
        kernel,
        out_shape=out_shape,
        in_specs=in_specs,
        out_specs=out_specs or jax.tree.map(lambda _: VMEM, out_shape),
        scratch_shapes=scratch,
        compiler_params=pltpu.CompilerParams(vmem_limit_bytes=vmem * 1024 * 1024),
        name=name,
    )


def fetch(pairs, sems, first):
    copies = [
        pltpu.make_async_copy(src, dst, sems.at[first + i]) for i, (src, dst) in enumerate(pairs)
    ]
    for copy in copies:
        copy.start()
    return copies


def columns_of(values, to, step):
    half = values.shape[0] // 2
    run = step // 2
    low = values[to * run : (to + 1) * run, :]
    return jnp.concatenate([low, values[half + to * run : half + (to + 1) * run, :]], axis=0)


def start_kernel(
    item_emb, user_emb, item_degree, user_degree, rows, cols, count, tiles, payload, message,
    items, users, item_deg, user_deg, slot_rows, slot_cols, live, held, base, sent_users, sems,
):
    share = message.shape[1]
    i_dev, emb = item_emb.shape
    u_dev = user_emb.shape[0]
    step = emb // share
    small = [
        (item_emb, items),
        (user_emb, users),
        (item_degree, item_deg),
        (user_degree, user_deg),
        (rows, slot_rows),
        (cols, slot_cols),
        (count, live),
    ]
    (fetched,) = fetch([(tiles, held)], sems, len(small))
    ready = fetch(small, sems, 0)
    fetched.wait()
    outgoing = fetch([(held, payload.at[pl.ds(share + 1, held.shape[0])])], sems, len(small) + 1)
    for copy in ready:
        copy.wait()
    values = jnp.concatenate(
        [
            items[...].astype(F32),
            users[...].astype(F32),
            jnp.zeros((BS - i_dev - u_dev, emb), F32),
        ],
        axis=0,
    ).T
    extra = jnp.concatenate(
        [
            item_deg[...],
            user_deg[...],
            slot_rows[0],
            slot_cols[0],
            live[...].reshape(1, 1),
            jnp.zeros((1, BS - i_dev - u_dev - 2 * NBLK - 1), jnp.int32),
        ],
        axis=1,
    ).astype(F32)
    base[share] = jnp.broadcast_to(extra, (step, BS)).astype(BF16)
    scale = lax.rsqrt(user_deg[...].astype(F32))
    for to in range(share):
        columns = columns_of(values, to, step)
        base[to] = columns.astype(BF16)
        sent = scale * columns[:, i_dev : i_dev + u_dev]
        quarter = message.shape[2]
        block = jnp.concatenate(
            [sent[p * quarter : (p + 1) * quarter, :] for p in range(share)], axis=1
        ).astype(BF16)
        sent_users[:, to] = jnp.broadcast_to(block[None], (message.shape[0], *block.shape))
    outgoing += fetch(
        [(base, payload.at[pl.ds(0, share + 1)]), (sent_users, message)], sems, len(small) + 2
    )
    for copy in outgoing:
        copy.wait()


def slot_list(place, slots, payloads):
    share = len(payloads)
    for away, payload in enumerate(payloads):
        x = lax.rem(place[1] + (share - away), share)
        step = payload.shape[1]
        blocks = BS // step
        for slot in range(NBLK):
            live = slot < slots[away, 2 * NBLK]
            first = share + 1 + slot * blocks
            tile = payload[first : first + blocks].reshape(BS, BS)
            yield x, slots[away, slot], slots[away, NBLK + slot], live, tile


def item_products(place, slots, payloads, users, acc):
    acc[...] = jnp.zeros_like(acc)
    for x, row, col, live, tile in slot_list(place, slots, payloads):
        prod = jnp.dot(users[row], tile, preferred_element_type=F32)
        acc[x, col] += jnp.where(live, prod, 0.0)


def items_one_kernel(
    place, slots, p0, p1, p2, p3, arrived, out, user_zero, user_scale, acc, users, base
):
    payloads = (p0, p1, p2, p3)
    tile_rows, share = arrived.shape[:2]
    step = users.shape[1]
    half = BS // 2
    u_dev = BS // share
    quarter = arrived.shape[2]
    group = lax.broadcasted_iota(jnp.int32, (quarter, BS), 1) // u_dev
    for row in range(tile_rows):
        blocks = [arrived[row, x].astype(F32) for x in range(share)]
        turned = []
        for away in range(share):
            mixed = blocks[0]
            for x in range(1, share):
                mixed = jnp.where(group == (x - away) % share, blocks[x], mixed)
            turned.append(pltpu.roll(mixed, away * u_dev, 1) if away else mixed)
        parts = []
        for p in range(share):
            part = turned[-p % share]
            for x in range(1, share):
                part = jnp.where(group == x, turned[(x - p) % share], part)
            parts.append(part)
        users[row] = jnp.concatenate(parts, axis=0).astype(BF16)

    lane = lax.broadcasted_iota(jnp.int32, (step, BS), 1)
    zero = jnp.zeros((step, BS), F32)
    degree = jnp.ones((step, BS), F32)
    for away, payload in enumerate(payloads):
        x = lax.rem(place[1] + (share - away), share)
        values, extra = payload[place[1]], payload[share]
        base[x, 0], base[x, 1] = values, extra
        piece = values.astype(F32)[:, half : half + u_dev]
        zero = jnp.where(lane // u_dev == x, jnp.concatenate([piece] * share, axis=1), zero)
        piece = extra.astype(F32)[:, half : half + u_dev]
        degree = jnp.where(lane // u_dev == x, jnp.concatenate([piece] * share, axis=1), degree)
    user_zero[...] = zero
    user_scale[...] = lax.rsqrt(degree)

    item_products(place, slots, payloads, users, acc)
    tile_cols = acc.shape[1]
    for x in range(share):
        for col in range(tile_cols):
            out[x * tile_cols + col] = acc[x, col].astype(BF16)
    first_block = share * tile_cols
    for pair in range(share // 2):
        first, degree = (
            jnp.concatenate(
                [base[2 * pair + k, part].astype(F32)[:, :half] for k in range(2)], axis=1
            )
            for part in range(2)
        )
        out[first_block + pair] = (lax.rsqrt(degree) * first).astype(BF16)
        out[first_block + share // 2 + pair] = degree.astype(BF16)


def users_kernel(place, slots, p0, p1, p2, p3, gathered, out, item_sum, acc, sent):
    share, tile_cols, step = item_sum.shape[:3]
    n_row = gathered.shape[0]
    half = BS // 2
    base = share * tile_cols

    def of_tile(block, x, col):
        pair, side = block + x // 2, (x % 2) * half
        return jnp.concatenate(
            [gathered[2 * col + k, pair].astype(F32)[:, side : side + half] for k in range(2)],
            axis=1,
        )

    for x in range(share):
        for col in range(tile_cols):
            at = x * tile_cols + col
            total = gathered[0, at].astype(F32)
            for part in range(1, n_row):
                total = total + gathered[part, at].astype(F32)
            item_sum[x, col] = total
            scale = lax.rsqrt(of_tile(base + share // 2, x, col))
            sent[x, col, :step] = of_tile(base, x, col).astype(BF16)
            sent[x, col, step:] = (scale * (scale * total)).astype(BF16)
    acc[...] = jnp.zeros_like(acc)
    for x, row, col, live, tile in slot_list(place, slots, (p0, p1, p2, p3)):
        prod = lax.dot_general(
            sent[x, col], tile, (((1,), (1,)), ((), ())), preferred_element_type=F32
        )
        acc[row] += jnp.where(live, prod, 0.0)
    out[...] = acc[...].astype(BF16)


def users_sum_kernel(parts, user_zero, user_scale, message, user_final):
    step = message.shape[1]
    total = parts[0].astype(F32)
    for part in range(1, parts.shape[0]):
        total = total + parts[part].astype(F32)
    scale = user_scale[...]
    users_one = scale * total[:step]
    users_two = scale * total[step:]
    message[...] = jnp.broadcast_to((scale * users_one).astype(BF16)[None], message.shape)
    user_final[...] = (user_zero[...] + users_one + users_two) / 3.0


def items_two_kernel(
    place, slots, p0, p1, p2, p3, users, item_sum, user_final, out, acc
):
    item_products(place, slots, (p0, p1, p2, p3), users, acc)
    share, tile_cols, step = acc.shape[:3]
    n_row = 2 * tile_cols
    half = BS // 2
    u_dev = BS // share
    run, quarter = step // 2, step // 4
    for x in range(share):
        own = user_final[...][:, x * u_dev : (x + 1) * u_dev]
        own = jnp.concatenate(
            [own[p * quarter : (p + 1) * quarter, :] for p in range(4)], axis=1
        )
        for col in range(tile_cols):
            total = acc[x, col] + item_sum[x, col] * (1.0 / n_row)
            for k in range(2):
                side = total[:, k * half : (k + 1) * half]
                block = jnp.concatenate([side[:run, :], side[run:, :]], axis=1).astype(BF16)
                out[2 * col + k, x, 0] = block[:quarter, :]
                out[2 * col + k, x, 1] = block[quarter:, :]
                mine = place[0] == 2 * col + k
                out[2 * col + k, x, 2] = jnp.where(mine, own, 0.0).astype(BF16)


def final_kernel(arrived, payload, item_final, user_final):
    n_row, share = arrived.shape[:2]
    i_dev, emb = item_final.shape
    u_dev = user_final.shape[0]
    total = arrived[0].astype(F32)
    for part in range(1, n_row):
        total = total + arrived[part].astype(F32)
    run, quarter = emb // share // 2, emb // share // 4
    scale = lax.rsqrt(payload[share].astype(F32)[:1, :i_dev])
    scale = jnp.concatenate([scale, scale], axis=1)
    sums = jnp.concatenate([total[x, p] for x in range(share) for p in range(2)], axis=0)
    own = [payload[x].astype(F32)[:, :i_dev] for x in range(share)]
    own = [jnp.concatenate([one[:run], one[run:]], axis=1) for one in own]
    layers = (jnp.concatenate(own, axis=0) + scale * sums) / 3.0
    below = jnp.concatenate([total[x, 2] for x in range(share)], axis=0)
    pad = jnp.zeros((BS - sums.shape[0] - below.shape[0], BS), F32)
    both = jnp.concatenate([layers, below, pad], axis=0).T
    width = share * run
    layers = jnp.concatenate([both[:i_dev, :width], both[i_dev : 2 * i_dev, :width]], axis=1)
    item_final[...] = layers.astype(BF16)
    pieces = []
    for h in range(2):
        for x in range(share):
            for p in range(2):
                rows = slice((2 * h + p) * u_dev, (2 * h + p + 1) * u_dev)
                first = width + x * quarter
                pieces.append(both[rows, first : first + quarter])
    user_final[...] = jnp.concatenate(pieces, axis=1).astype(BF16)


def exchange(values, axes):
    return lax.all_to_all(values, axes, split_axis=0, concat_axis=0, tiled=True)


def per_device(
    user_emb, item_emb, user_degree, item_degree, block_values, block_row, block_col, block_count
):
    share = lax.axis_size("x")
    n_row = lax.axis_size(ROW)
    tile_rows = lax.axis_size(PLANE)
    n_col = tile_rows * share
    u_dev, emb = user_emb.shape
    i_dev = item_emb.shape[0]
    tile_cols = i_dev * n_row // BS
    step = emb // share
    shape = jax.ShapeDtypeStruct
    acc_items = pltpu.VMEM((share, tile_cols, step, BS), F32)

    item_degree = item_degree.reshape(1, i_dev)
    held = NBLK * BS // step
    payload, message = call(
        start_kernel,
        "start",
        (shape((share + 1 + held, step, BS), BF16), shape((tile_rows, share, step // share, BS), BF16)),
        [HBM] * 8,
        [
            pltpu.VMEM((i_dev, emb), BF16),
            pltpu.VMEM((u_dev, emb), BF16),
            pltpu.VMEM((1, i_dev), jnp.int32),
            pltpu.VMEM((1, u_dev), jnp.int32),
            pltpu.VMEM((1, 1, NBLK), jnp.int32),
            pltpu.VMEM((1, 1, NBLK), jnp.int32),
            pltpu.VMEM((1,), jnp.int32),
            pltpu.VMEM((held, step, BS), BF16),
            pltpu.VMEM((share + 1, step, BS), BF16),
            pltpu.VMEM((tile_rows, share, step // share, BS), BF16),
            pltpu.SemaphoreType.DMA((11,)),
        ],
        (HBM, HBM),
        vmem=60,
    )(
        item_emb, user_emb, item_degree, user_degree.reshape(1, u_dev), block_row, block_col,
        block_count.reshape(1), block_values.reshape(held, step, BS),
    )
    with jax.named_scope("sent_users_0"):
        arrived = exchange(message.reshape(n_col, step // share, BS), PLANE + ("x",))
    with jax.named_scope("payloads_along_x"):
        payloads = [payload] + [
            lax.ppermute(payload, "x", [(x, (x + away) % share) for x in range(share)])
            for away in range(1, share)
        ]
    place = jnp.stack([lax.axis_index(ROW), lax.axis_index("x")]).astype(jnp.int32)
    first_slot = i_dev + u_dev
    slots = jnp.stack(
        [one[share, 0, first_slot : first_slot + 2 * NBLK + 1] for one in payloads]
    ).astype(jnp.int32)
    slotted = [SMEM] * 2 + [VMEM] * share
    slot_args = (place, slots, *payloads)
    blocks = share * tile_cols + share
    first_shape = message.shape
    message, user_zero, user_scale = call(
        items_one_kernel,
        "items_1_parts",
        (shape((blocks, step, BS), BF16), shape((step, BS), F32), shape((step, BS), F32)),
        slotted + [VMEM],
        [
            acc_items,
            pltpu.VMEM((tile_rows, step, BS), BF16),
            pltpu.VMEM((share, 2, step, BS), BF16),
        ],
    )(*slot_args, arrived.reshape(first_shape))
    with jax.named_scope("items_0_and_1"):
        gathered = lax.all_gather(message, ROW, axis=0)
    message, item_sum = call(
        users_kernel,
        "users_1_and_2_parts",
        (shape((tile_rows, 2 * step, BS), BF16), shape((share, tile_cols, step, BS), F32)),
        slotted + [VMEM],
        [
            pltpu.VMEM((tile_rows, 2 * step, BS), F32),
            pltpu.VMEM((share, tile_cols, 2 * step, BS), BF16),
        ],
    )(*slot_args, gathered)
    with jax.named_scope("users_1_and_2"):
        parts = exchange(message, PLANE)
    message, user_final = call(
        users_sum_kernel,
        "users_sum",
        (shape((tile_rows, step, BS), BF16), shape((step, BS), F32)),
        [VMEM] * 3,
    )(parts, user_zero, user_scale)
    with jax.named_scope("sent_users_1"):
        users = exchange(message, PLANE)
    message = call(
        items_two_kernel,
        "items_2_parts",
        shape((n_row, share, 3, step // 4, BS), BF16),
        slotted + [VMEM] * 3,
        [acc_items],
    )(*slot_args, users, item_sum, user_final)
    with jax.named_scope("items_2"):
        parts = exchange(message.reshape(n_row * share, *message.shape[2:]), ROW + ("x",))
    item_final, user_final = call(
        final_kernel,
        "final",
        (shape((i_dev, emb), BF16), shape((u_dev, emb), BF16)),
        [VMEM, VMEM],
    )(parts.reshape(message.shape), payload)
    return user_final, item_final


def solution(mesh):
    fine = Mesh(mesh.devices.reshape(4, 2, 4, 8, 4), AXES)
    col = PLANE + ("x",)
    in_specs = (
        P(AXES, None),
        P(AXES, None),
        P(AXES),
        P(AXES),
        P(ROW, col, None, None, None),
        P(ROW, col, None),
        P(ROW, col, None),
        P(ROW, col),
    )
    out_specs = (P(AXES, None), P(AXES, None))
    return jax.shard_map(
        per_device, mesh=fine, in_specs=in_specs, out_specs=out_specs, check_vma=False
    )
```

```python
import jax
import jax.numpy as jnp
from jax import lax
from jax.experimental import pallas as pl
from jax.experimental.pallas import tpu as pltpu
from jax.sharding import Mesh, PartitionSpec as P

BS = 128
NBLK = 8
F32 = jnp.float32
BF16 = jnp.bfloat16
ROW = ("zh", "co")
PLANE = ("zl", "y")
AXES = ROW + PLANE + ("x",)

VMEM = pl.BlockSpec(memory_space=pltpu.VMEM)
HBM = pl.BlockSpec(memory_space=pltpu.HBM)
SMEM = pl.BlockSpec(memory_space=pltpu.SMEM)


def call(kernel, name, out_shape, in_specs, scratch=(), out_specs=None, vmem=24):
    return pl.pallas_call(
        kernel,
        out_shape=out_shape,
        in_specs=in_specs,
        out_specs=out_specs or jax.tree.map(lambda _: VMEM, out_shape),
        scratch_shapes=scratch,
        compiler_params=pltpu.CompilerParams(vmem_limit_bytes=vmem * 1024 * 1024),
        name=name,
    )


def fetch(pairs, sems, first):
    copies = [
        pltpu.make_async_copy(src, dst, sems.at[first + i]) for i, (src, dst) in enumerate(pairs)
    ]
    for copy in copies:
        copy.start()
    return copies


def columns_of(values, to, step):
    half = values.shape[0] // 2
    run = step // 2
    low = values[to * run : (to + 1) * run, :]
    return jnp.concatenate([low, values[half + to * run : half + (to + 1) * run, :]], axis=0)


def start_kernel(
    item_emb, user_emb, item_degree, user_degree, rows, cols, count, tiles, payload, message,
    items, users, item_deg, user_deg, slot_rows, slot_cols, live, held, base, sent_users, sems,
):
    share = message.shape[1]
    i_dev, emb = item_emb.shape
    u_dev = user_emb.shape[0]
    step = emb // share
    small = [
        (item_emb, items),
        (user_emb, users),
        (item_degree, item_deg),
        (user_degree, user_deg),
        (rows, slot_rows),
        (cols, slot_cols),
        (count, live),
    ]
    (fetched,) = fetch([(tiles, held)], sems, len(small))
    ready = fetch(small, sems, 0)
    fetched.wait()
    outgoing = fetch([(held, payload.at[pl.ds(share + 1, held.shape[0])])], sems, len(small) + 1)
    for copy in ready:
        copy.wait()
    values = jnp.concatenate(
        [
            items[...].astype(F32),
            users[...].astype(F32),
            jnp.zeros((BS - i_dev - u_dev, emb), F32),
        ],
        axis=0,
    ).T
    extra = jnp.concatenate(
        [
            item_deg[...],
            user_deg[...],
            slot_rows[0],
            slot_cols[0],
            live[...].reshape(1, 1),
            jnp.zeros((1, BS - i_dev - u_dev - 2 * NBLK - 1), jnp.int32),
        ],
        axis=1,
    ).astype(F32)
    base[share] = jnp.broadcast_to(extra, (step, BS)).astype(BF16)
    scale = lax.rsqrt(user_deg[...].astype(F32))
    for to in range(share):
        columns = columns_of(values, to, step)
        base[to] = columns.astype(BF16)
        sent = scale * columns[:, i_dev : i_dev + u_dev]
        quarter = message.shape[2]
        block = jnp.concatenate(
            [sent[p * quarter : (p + 1) * quarter, :] for p in range(share)], axis=1
        ).astype(BF16)
        sent_users[:, to] = jnp.broadcast_to(block[None], (message.shape[0], *block.shape))
    outgoing += fetch(
        [(base, payload.at[pl.ds(0, share + 1)]), (sent_users, message)], sems, len(small) + 2
    )
    for copy in outgoing:
        copy.wait()


def slot_list(place, slots, payloads):
    share = len(payloads)
    for away, payload in enumerate(payloads):
        x = lax.bitwise_xor(place[1], away)
        step = payload.shape[1]
        blocks = BS // step
        for slot in range(NBLK):
            live = slot < slots[away, 2 * NBLK]
            first = share + 1 + slot * blocks
            tile = payload[first : first + blocks].reshape(BS, BS)
            yield x, slots[away, slot], slots[away, NBLK + slot], live, tile


def item_products(place, slots, payloads, users, acc):
    acc[...] = jnp.zeros_like(acc)
    for x, row, col, live, tile in slot_list(place, slots, payloads):
        prod = jnp.dot(users[row], tile, preferred_element_type=F32)
        acc[x, col] += jnp.where(live, prod, 0.0)


def items_one_kernel(
    place, slots, p0, p1, p2, p3, arrived, out, user_zero, user_scale, acc, users, base
):
    payloads = (p0, p1, p2, p3)
    tile_rows, share = arrived.shape[:2]
    step = users.shape[1]
    half = BS // 2
    u_dev = BS // share
    quarter = arrived.shape[2]
    group = lax.broadcasted_iota(jnp.int32, (quarter, BS), 1) // u_dev
    for row in range(tile_rows):
        blocks = [arrived[row, x].astype(F32) for x in range(share)]
        turned = []
        for away in range(share):
            mixed = blocks[0]
            for x in range(1, share):
                mixed = jnp.where(group == (x - away) % share, blocks[x], mixed)
            turned.append(pltpu.roll(mixed, away * u_dev, 1) if away else mixed)
        parts = []
        for p in range(share):
            part = turned[-p % share]
            for x in range(1, share):
                part = jnp.where(group == x, turned[(x - p) % share], part)
            parts.append(part)
        users[row] = jnp.concatenate(parts, axis=0).astype(BF16)

    lane = lax.broadcasted_iota(jnp.int32, (step, BS), 1)
    zero = jnp.zeros((step, BS), F32)
    degree = jnp.ones((step, BS), F32)
    for away, payload in enumerate(payloads):
        x = lax.bitwise_xor(place[1], away)
        values, extra = payload[place[1]], payload[share]
        base[x, 0], base[x, 1] = values, extra
        piece = values.astype(F32)[:, half : half + u_dev]
        zero = jnp.where(lane // u_dev == x, jnp.concatenate([piece] * share, axis=1), zero)
        piece = extra.astype(F32)[:, half : half + u_dev]
        degree = jnp.where(lane // u_dev == x, jnp.concatenate([piece] * share, axis=1), degree)
    user_zero[...] = zero
    user_scale[...] = lax.rsqrt(degree)

    item_products(place, slots, payloads, users, acc)
    tile_cols = acc.shape[1]
    for x in range(share):
        for col in range(tile_cols):
            out[x * tile_cols + col] = acc[x, col].astype(BF16)
    first_block = share * tile_cols
    for pair in range(share // 2):
        first, degree = (
            jnp.concatenate(
                [base[2 * pair + k, part].astype(F32)[:, :half] for k in range(2)], axis=1
            )
            for part in range(2)
        )
        out[first_block + pair] = (lax.rsqrt(degree) * first).astype(BF16)
        out[first_block + share // 2 + pair] = degree.astype(BF16)


def users_kernel(place, slots, p0, p1, p2, p3, gathered, out, item_sum, acc, sent):
    share, tile_cols, step = item_sum.shape[:3]
    n_row = gathered.shape[0]
    half = BS // 2
    base = share * tile_cols

    def of_tile(block, x, col):
        pair, side = block + x // 2, (x % 2) * half
        return jnp.concatenate(
            [gathered[2 * col + k, pair].astype(F32)[:, side : side + half] for k in range(2)],
            axis=1,
        )

    for x in range(share):
        for col in range(tile_cols):
            at = x * tile_cols + col
            total = gathered[0, at].astype(F32)
            for part in range(1, n_row):
                total = total + gathered[part, at].astype(F32)
            item_sum[x, col] = total
            scale = lax.rsqrt(of_tile(base + share // 2, x, col))
            sent[x, col, :step] = of_tile(base, x, col).astype(BF16)
            sent[x, col, step:] = (scale * (scale * total)).astype(BF16)
    acc[...] = jnp.zeros_like(acc)
    for x, row, col, live, tile in slot_list(place, slots, (p0, p1, p2, p3)):
        prod = lax.dot_general(
            sent[x, col], tile, (((1,), (1,)), ((), ())), preferred_element_type=F32
        )
        acc[row] += jnp.where(live, prod, 0.0)
    out[...] = acc[...].astype(BF16)


def users_sum_kernel(parts, user_zero, user_scale, message, user_final):
    step = message.shape[1]
    total = parts[0].astype(F32)
    for part in range(1, parts.shape[0]):
        total = total + parts[part].astype(F32)
    scale = user_scale[...]
    users_one = scale * total[:step]
    users_two = scale * total[step:]
    message[...] = jnp.broadcast_to((scale * users_one).astype(BF16)[None], message.shape)
    user_final[...] = (user_zero[...] + users_one + users_two) / 3.0


def items_two_kernel(
    place, slots, p0, p1, p2, p3, users, item_sum, user_final, out, acc
):
    item_products(place, slots, (p0, p1, p2, p3), users, acc)
    share, tile_cols, step = acc.shape[:3]
    n_row = 2 * tile_cols
    half = BS // 2
    u_dev = BS // share
    run, quarter = step // 2, step // 4
    for x in range(share):
        own = user_final[...][:, x * u_dev : (x + 1) * u_dev]
        own = jnp.concatenate(
            [own[p * quarter : (p + 1) * quarter, :] for p in range(4)], axis=1
        )
        for col in range(tile_cols):
            total = acc[x, col] + item_sum[x, col] * (1.0 / n_row)
            for k in range(2):
                side = total[:, k * half : (k + 1) * half]
                block = jnp.concatenate([side[:run, :], side[run:, :]], axis=1).astype(BF16)
                out[x, 2 * col + k, 0] = block[:quarter, :]
                out[x, 2 * col + k, 1] = block[quarter:, :]
                mine = place[0] == 2 * col + k
                out[x, 2 * col + k, 2] = jnp.where(mine, own, 0.0).astype(BF16)


def final_kernel(arrived, payload, item_final, user_final):
    share, n_row = arrived.shape[:2]
    i_dev, emb = item_final.shape
    u_dev = user_final.shape[0]
    total = arrived[:, 0].astype(F32)
    for part in range(1, n_row):
        total = total + arrived[:, part].astype(F32)
    run, quarter = emb // share // 2, emb // share // 4
    scale = lax.rsqrt(payload[share].astype(F32)[:1, :i_dev])
    scale = jnp.concatenate([scale, scale], axis=1)
    sums = jnp.concatenate([total[x, p] for x in range(share) for p in range(2)], axis=0)
    own = [payload[x].astype(F32)[:, :i_dev] for x in range(share)]
    own = [jnp.concatenate([one[:run], one[run:]], axis=1) for one in own]
    layers = (jnp.concatenate(own, axis=0) + scale * sums) / 3.0
    below = jnp.concatenate([total[x, 2] for x in range(share)], axis=0)
    pad = jnp.zeros((BS - sums.shape[0] - below.shape[0], BS), F32)
    both = jnp.concatenate([layers, below, pad], axis=0).T
    width = share * run
    layers = jnp.concatenate([both[:i_dev, :width], both[i_dev : 2 * i_dev, :width]], axis=1)
    item_final[...] = layers.astype(BF16)
    pieces = []
    for h in range(2):
        for x in range(share):
            for p in range(2):
                rows = slice((2 * h + p) * u_dev, (2 * h + p + 1) * u_dev)
                first = width + x * quarter
                pieces.append(both[rows, first : first + quarter])
    user_final[...] = jnp.concatenate(pieces, axis=1).astype(BF16)


def exchange(values, axes):
    return lax.all_to_all(values, axes, split_axis=0, concat_axis=0, tiled=True)


def per_device(
    user_emb, item_emb, user_degree, item_degree, block_values, block_row, block_col, block_count
):
    share = lax.axis_size("x")
    n_row = lax.axis_size(ROW)
    tile_rows = lax.axis_size(PLANE)
    n_col = tile_rows * share
    u_dev, emb = user_emb.shape
    i_dev = item_emb.shape[0]
    tile_cols = i_dev * n_row // BS
    step = emb // share
    shape = jax.ShapeDtypeStruct
    acc_items = pltpu.VMEM((share, tile_cols, step, BS), F32)

    item_degree = item_degree.reshape(1, i_dev)
    held = NBLK * BS // step
    payload, message = call(
        start_kernel,
        "start",
        (shape((share + 1 + held, step, BS), BF16), shape((tile_rows, share, step // share, BS), BF16)),
        [HBM] * 8,
        [
            pltpu.VMEM((i_dev, emb), BF16),
            pltpu.VMEM((u_dev, emb), BF16),
            pltpu.VMEM((1, i_dev), jnp.int32),
            pltpu.VMEM((1, u_dev), jnp.int32),
            pltpu.VMEM((1, 1, NBLK), jnp.int32),
            pltpu.VMEM((1, 1, NBLK), jnp.int32),
            pltpu.VMEM((1,), jnp.int32),
            pltpu.VMEM((held, step, BS), BF16),
            pltpu.VMEM((share + 1, step, BS), BF16),
            pltpu.VMEM((tile_rows, share, step // share, BS), BF16),
            pltpu.SemaphoreType.DMA((11,)),
        ],
        (HBM, HBM),
        vmem=60,
    )(
        item_emb, user_emb, item_degree, user_degree.reshape(1, u_dev), block_row, block_col,
        block_count.reshape(1), block_values.reshape(held, step, BS),
    )
    with jax.named_scope("sent_users_0"):
        arrived = exchange(message.reshape(n_col, step // share, BS), PLANE + ("x",))
    with jax.named_scope("payloads_along_x"):
        payloads = [payload] + [
            lax.ppermute(payload, "x", [(x, x ^ away) for x in range(share)])
            for away in range(1, share)
        ]
    place = jnp.stack([lax.axis_index(ROW), lax.axis_index("x")]).astype(jnp.int32)
    first_slot = i_dev + u_dev
    slots = jnp.stack(
        [one[share, 0, first_slot : first_slot + 2 * NBLK + 1] for one in payloads]
    ).astype(jnp.int32)
    slotted = [SMEM] * 2 + [VMEM] * share
    slot_args = (place, slots, *payloads)
    blocks = share * tile_cols + share
    first_shape = message.shape
    message, user_zero, user_scale = call(
        items_one_kernel,
        "items_1_parts",
        (shape((blocks, step, BS), BF16), shape((step, BS), F32), shape((step, BS), F32)),
        slotted + [VMEM],
        [
            acc_items,
            pltpu.VMEM((tile_rows, step, BS), BF16),
            pltpu.VMEM((share, 2, step, BS), BF16),
        ],
    )(*slot_args, arrived.reshape(first_shape))
    with jax.named_scope("items_0_and_1"):
        gathered = lax.all_gather(message, ROW, axis=0)
    message, item_sum = call(
        users_kernel,
        "users_1_and_2_parts",
        (shape((tile_rows, 2 * step, BS), BF16), shape((share, tile_cols, step, BS), F32)),
        slotted + [VMEM],
        [
            pltpu.VMEM((tile_rows, 2 * step, BS), F32),
            pltpu.VMEM((share, tile_cols, 2 * step, BS), BF16),
        ],
    )(*slot_args, gathered)
    with jax.named_scope("users_1_and_2"):
        parts = exchange(message, PLANE)
    message, user_final = call(
        users_sum_kernel,
        "users_sum",
        (shape((tile_rows, step, BS), BF16), shape((step, BS), F32)),
        [VMEM] * 3,
    )(parts, user_zero, user_scale)
    with jax.named_scope("sent_users_1"):
        users = exchange(message, PLANE)
    message = call(
        items_two_kernel,
        "items_2_parts",
        shape((share, n_row, 3, step // 4, BS), BF16),
        slotted + [VMEM] * 3,
        [acc_items],
    )(*slot_args, users, item_sum, user_final)
    with jax.named_scope("items_2"):
        parts = exchange(message.reshape(n_row * share, *message.shape[2:]), ("x",) + ROW)
    item_final, user_final = call(
        final_kernel,
        "final",
        (shape((i_dev, emb), BF16), shape((u_dev, emb), BF16)),
        [VMEM, VMEM],
    )(parts.reshape(message.shape), payload)
    return user_final, item_final


def solution(mesh):
    fine = Mesh(mesh.devices.reshape(4, 2, 4, 8, 4), AXES)
    col = PLANE + ("x",)
    in_specs = (
        P(AXES, None),
        P(AXES, None),
        P(AXES),
        P(AXES),
        P(ROW, col, None, None, None),
        P(ROW, col, None),
        P(ROW, col, None),
        P(ROW, col),
    )
    out_specs = (P(AXES, None), P(AXES, None))
    return jax.shard_map(
        per_device, mesh=fine, in_specs=in_specs, out_specs=out_specs, check_vma=False
    )
```

```python
import jax
import jax.numpy as jnp
from jax import lax
from jax.experimental import pallas as pl
from jax.experimental.pallas import tpu as pltpu
from jax.sharding import Mesh, PartitionSpec as P

BS = 128
NBLK = 8
F32 = jnp.float32
BF16 = jnp.bfloat16
ROW = ("zh", "co")
PLANE = ("zl", "y")
AXES = ROW + PLANE + ("x",)

VMEM = pl.BlockSpec(memory_space=pltpu.VMEM)
HBM = pl.BlockSpec(memory_space=pltpu.HBM)
SMEM = pl.BlockSpec(memory_space=pltpu.SMEM)


def call(kernel, name, out_shape, in_specs, scratch=(), out_specs=None, vmem=24):
    return pl.pallas_call(
        kernel,
        out_shape=out_shape,
        in_specs=in_specs,
        out_specs=out_specs or jax.tree.map(lambda _: VMEM, out_shape),
        scratch_shapes=scratch,
        compiler_params=pltpu.CompilerParams(vmem_limit_bytes=vmem * 1024 * 1024),
        name=name,
    )


def fetch(pairs, sems, first):
    copies = [
        pltpu.make_async_copy(src, dst, sems.at[first + i]) for i, (src, dst) in enumerate(pairs)
    ]
    for copy in copies:
        copy.start()
    return copies


def columns_of(values, to, step):
    half = values.shape[0] // 2
    run = step // 2
    low = values[to * run : (to + 1) * run, :]
    return jnp.concatenate([low, values[half + to * run : half + (to + 1) * run, :]], axis=0)


def start_kernel(
    item_emb, user_emb, item_degree, user_degree, rows, cols, count, tiles, payload, message,
    items, users, item_deg, user_deg, slot_rows, slot_cols, live, held, base, sent_users, sems,
):
    share = message.shape[1]
    i_dev, emb = item_emb.shape
    u_dev = user_emb.shape[0]
    step = emb // share
    small = [
        (item_emb, items),
        (user_emb, users),
        (item_degree, item_deg),
        (user_degree, user_deg),
        (rows, slot_rows),
        (cols, slot_cols),
        (count, live),
    ]
    (fetched,) = fetch([(tiles, held)], sems, len(small))
    ready = fetch(small, sems, 0)
    fetched.wait()
    outgoing = fetch([(held, payload.at[pl.ds(share + 1, held.shape[0])])], sems, len(small) + 1)
    for copy in ready:
        copy.wait()
    values = jnp.concatenate(
        [
            items[...].astype(F32),
            users[...].astype(F32),
            jnp.zeros((BS - i_dev - u_dev, emb), F32),
        ],
        axis=0,
    ).T
    extra = jnp.concatenate(
        [
            item_deg[...],
            user_deg[...],
            slot_rows[0],
            slot_cols[0],
            live[...].reshape(1, 1),
            jnp.zeros((1, BS - i_dev - u_dev - 2 * NBLK - 1), jnp.int32),
        ],
        axis=1,
    ).astype(F32)
    base[share] = jnp.broadcast_to(extra, (step, BS)).astype(BF16)
    scale = lax.rsqrt(user_deg[...].astype(F32))
    for to in range(share):
        columns = columns_of(values, to, step)
        base[to] = columns.astype(BF16)
        sent = scale * columns[:, i_dev : i_dev + u_dev]
        quarter = message.shape[2]
        block = jnp.concatenate(
            [sent[p * quarter : (p + 1) * quarter, :] for p in range(share)], axis=1
        ).astype(BF16)
        sent_users[:, to] = jnp.broadcast_to(block[None], (message.shape[0], *block.shape))
    outgoing += fetch(
        [(base, payload.at[pl.ds(0, share + 1)]), (sent_users, message)], sems, len(small) + 2
    )
    for copy in outgoing:
        copy.wait()


def slot_list(place, slots, payloads):
    share = len(payloads)
    for away, payload in enumerate(payloads):
        x = lax.rem(place[1] + (share - away), share)
        step = payload.shape[1]
        blocks = BS // step
        for slot in range(NBLK):
            live = slot < slots[away, 2 * NBLK]
            first = share + 1 + slot * blocks
            tile = payload[first : first + blocks].reshape(BS, BS)
            yield x, slots[away, slot], slots[away, NBLK + slot], live, tile


def item_products(place, slots, payloads, users, acc):
    acc[...] = jnp.zeros_like(acc)
    for x, row, col, live, tile in slot_list(place, slots, payloads):
        prod = jnp.dot(users[row], tile, preferred_element_type=F32)
        acc[x, col] += jnp.where(live, prod, 0.0)


def items_one_kernel(
    place, slots, p0, p1, p2, p3, arrived, out, user_zero, user_scale, acc, users, base
):
    payloads = (p0, p1, p2, p3)
    tile_rows, share = arrived.shape[:2]
    step = users.shape[1]
    half = BS // 2
    u_dev = BS // share
    quarter = arrived.shape[2]
    group = lax.broadcasted_iota(jnp.int32, (quarter, BS), 1) // u_dev
    for row in range(tile_rows):
        blocks = [arrived[row, x].astype(F32) for x in range(share)]
        turned = []
        for away in range(share):
            mixed = blocks[0]
            for x in range(1, share):
                mixed = jnp.where(group == (x - away) % share, blocks[x], mixed)
            turned.append(pltpu.roll(mixed, away * u_dev, 1) if away else mixed)
        parts = []
        for p in range(share):
            part = turned[-p % share]
            for x in range(1, share):
                part = jnp.where(group == x, turned[(x - p) % share], part)
            parts.append(part)
        users[row] = jnp.concatenate(parts, axis=0).astype(BF16)

    lane = lax.broadcasted_iota(jnp.int32, (step, BS), 1)
    zero = jnp.zeros((step, BS), F32)
    degree = jnp.ones((step, BS), F32)
    for away, payload in enumerate(payloads):
        x = lax.rem(place[1] + (share - away), share)
        values, extra = payload[place[1]], payload[share]
        base[x, 0], base[x, 1] = values, extra
        piece = values.astype(F32)[:, half : half + u_dev]
        zero = jnp.where(lane // u_dev == x, jnp.concatenate([piece] * share, axis=1), zero)
        piece = extra.astype(F32)[:, half : half + u_dev]
        degree = jnp.where(lane // u_dev == x, jnp.concatenate([piece] * share, axis=1), degree)
    user_zero[...] = zero
    user_scale[...] = lax.rsqrt(degree)

    item_products(place, slots, payloads, users, acc)
    tile_cols = acc.shape[1]
    for x in range(share):
        for col in range(tile_cols):
            out[x * tile_cols + col] = acc[x, col].astype(BF16)
    first_block = share * tile_cols
    degrees = []
    for pair in range(share // 2):
        first, degree = (
            jnp.concatenate(
                [base[2 * pair + k, part].astype(F32)[:, :half] for k in range(2)], axis=1
            )
            for part in range(2)
        )
        out[first_block + pair] = (lax.rsqrt(degree) * first).astype(BF16)
        degrees.append(degree[: step // 2])
    out[first_block + share // 2] = jnp.concatenate(degrees, axis=0).astype(BF16)


def users_kernel(place, slots, p0, p1, p2, p3, gathered, out, item_sum, acc, sent):
    share, tile_cols, step = item_sum.shape[:3]
    n_row = gathered.shape[0]
    half = BS // 2
    base = share * tile_cols

    def of_tile(block, x, col):
        pair, side = block + x // 2, (x % 2) * half
        return jnp.concatenate(
            [gathered[2 * col + k, pair].astype(F32)[:, side : side + half] for k in range(2)],
            axis=1,
        )

    for x in range(share):
        for col in range(tile_cols):
            at = x * tile_cols + col
            total = gathered[0, at].astype(F32)
            for part in range(1, n_row):
                total = total + gathered[part, at].astype(F32)
            item_sum[x, col] = total
            line, side = (x // 2) * (step // 2), (x % 2) * half
            scale = lax.rsqrt(
                jnp.concatenate(
                    [
                        gathered[2 * col + k, base + share // 2].astype(F32)[
                            line : line + 1, side : side + half
                        ]
                        for k in range(2)
                    ],
                    axis=1,
                )
            )
            sent[x, col, :step] = of_tile(base, x, col).astype(BF16)
            sent[x, col, step:] = (scale * (scale * total)).astype(BF16)
    acc[...] = jnp.zeros_like(acc)
    for x, row, col, live, tile in slot_list(place, slots, (p0, p1, p2, p3)):
        prod = lax.dot_general(
            sent[x, col], tile, (((1,), (1,)), ((), ())), preferred_element_type=F32
        )
        acc[row] += jnp.where(live, prod, 0.0)
    out[...] = acc[...].astype(BF16)


def users_sum_kernel(parts, user_zero, user_scale, message, user_final):
    step = message.shape[1]
    total = parts[0].astype(F32)
    for part in range(1, parts.shape[0]):
        total = total + parts[part].astype(F32)
    scale = user_scale[...]
    users_one = scale * total[:step]
    users_two = scale * total[step:]
    message[...] = jnp.broadcast_to((scale * users_one).astype(BF16)[None], message.shape)
    user_final[...] = (user_zero[...] + users_one + users_two) / 3.0


def items_two_kernel(
    place, slots, p0, p1, p2, p3, users, item_sum, user_final, out, acc
):
    item_products(place, slots, (p0, p1, p2, p3), users, acc)
    share, tile_cols, step = acc.shape[:3]
    n_row = 2 * tile_cols
    half = BS // 2
    u_dev = BS // share
    run, quarter = step // 2, step // 4
    for x in range(share):
        own = user_final[...][:, x * u_dev : (x + 1) * u_dev]
        own = jnp.concatenate(
            [own[p * quarter : (p + 1) * quarter, :] for p in range(4)], axis=1
        )
        for col in range(tile_cols):
            total = acc[x, col] + item_sum[x, col] * (1.0 / n_row)
            for k in range(2):
                side = total[:, k * half : (k + 1) * half]
                block = jnp.concatenate([side[:run, :], side[run:, :]], axis=1).astype(BF16)
                out[2 * col + k, x, 0] = block[:quarter, :]
                out[2 * col + k, x, 1] = block[quarter:, :]
                mine = place[0] == 2 * col + k
                out[2 * col + k, x, 2] = jnp.where(mine, own, 0.0).astype(BF16)


def final_kernel(arrived, payload, item_final, user_final):
    n_row, share = arrived.shape[:2]
    i_dev, emb = item_final.shape
    u_dev = user_final.shape[0]
    total = arrived[0].astype(F32)
    for part in range(1, n_row):
        total = total + arrived[part].astype(F32)
    run, quarter = emb // share // 2, emb // share // 4
    scale = lax.rsqrt(payload[share].astype(F32)[:1, :i_dev])
    scale = jnp.concatenate([scale, scale], axis=1)
    sums = jnp.concatenate([total[x, p] for x in range(share) for p in range(2)], axis=0)
    own = [payload[x].astype(F32)[:, :i_dev] for x in range(share)]
    own = [jnp.concatenate([one[:run], one[run:]], axis=1) for one in own]
    layers = (jnp.concatenate(own, axis=0) + scale * sums) / 3.0
    below = jnp.concatenate([total[x, 2] for x in range(share)], axis=0)
    pad = jnp.zeros((BS - sums.shape[0] - below.shape[0], BS), F32)
    both = jnp.concatenate([layers, below, pad], axis=0).T
    width = share * run
    layers = jnp.concatenate([both[:i_dev, :width], both[i_dev : 2 * i_dev, :width]], axis=1)
    item_final[...] = layers.astype(BF16)
    pieces = []
    for h in range(2):
        for x in range(share):
            for p in range(2):
                rows = slice((2 * h + p) * u_dev, (2 * h + p + 1) * u_dev)
                first = width + x * quarter
                pieces.append(both[rows, first : first + quarter])
    user_final[...] = jnp.concatenate(pieces, axis=1).astype(BF16)


def exchange(values, axes):
    return lax.all_to_all(values, axes, split_axis=0, concat_axis=0, tiled=True)


def per_device(
    user_emb, item_emb, user_degree, item_degree, block_values, block_row, block_col, block_count
):
    share = lax.axis_size("x")
    n_row = lax.axis_size(ROW)
    tile_rows = lax.axis_size(PLANE)
    n_col = tile_rows * share
    u_dev, emb = user_emb.shape
    i_dev = item_emb.shape[0]
    tile_cols = i_dev * n_row // BS
    step = emb // share
    shape = jax.ShapeDtypeStruct
    acc_items = pltpu.VMEM((share, tile_cols, step, BS), F32)

    item_degree = item_degree.reshape(1, i_dev)
    held = NBLK * BS // step
    payload, message = call(
        start_kernel,
        "start",
        (shape((share + 1 + held, step, BS), BF16), shape((tile_rows, share, step // share, BS), BF16)),
        [HBM] * 8,
        [
            pltpu.VMEM((i_dev, emb), BF16),
            pltpu.VMEM((u_dev, emb), BF16),
            pltpu.VMEM((1, i_dev), jnp.int32),
            pltpu.VMEM((1, u_dev), jnp.int32),
            pltpu.VMEM((1, 1, NBLK), jnp.int32),
            pltpu.VMEM((1, 1, NBLK), jnp.int32),
            pltpu.VMEM((1,), jnp.int32),
            pltpu.VMEM((held, step, BS), BF16),
            pltpu.VMEM((share + 1, step, BS), BF16),
            pltpu.VMEM((tile_rows, share, step // share, BS), BF16),
            pltpu.SemaphoreType.DMA((11,)),
        ],
        (HBM, HBM),
        vmem=60,
    )(
        item_emb, user_emb, item_degree, user_degree.reshape(1, u_dev), block_row, block_col,
        block_count.reshape(1), block_values.reshape(held, step, BS),
    )
    with jax.named_scope("sent_users_0"):
        arrived = exchange(message.reshape(n_col, step // share, BS), PLANE + ("x",))
    with jax.named_scope("payloads_along_x"):
        payloads = [payload] + [
            lax.ppermute(payload, "x", [(x, (x + away) % share) for x in range(share)])
            for away in range(1, share)
        ]
    place = jnp.stack([lax.axis_index(ROW), lax.axis_index("x")]).astype(jnp.int32)
    first_slot = i_dev + u_dev
    slots = jnp.stack(
        [one[share, 0, first_slot : first_slot + 2 * NBLK + 1] for one in payloads]
    ).astype(jnp.int32)
    slotted = [SMEM] * 2 + [VMEM] * share
    slot_args = (place, slots, *payloads)
    blocks = share * tile_cols + share // 2 + 1
    first_shape = message.shape
    message, user_zero, user_scale = call(
        items_one_kernel,
        "items_1_parts",
        (shape((blocks, step, BS), BF16), shape((step, BS), F32), shape((step, BS), F32)),
        slotted + [VMEM],
        [
            acc_items,
            pltpu.VMEM((tile_rows, step, BS), BF16),
            pltpu.VMEM((share, 2, step, BS), BF16),
        ],
    )(*slot_args, arrived.reshape(first_shape))
    with jax.named_scope("items_0_and_1"):
        gathered = lax.all_gather(message, ROW, axis=0)
    message, item_sum = call(
        users_kernel,
        "users_1_and_2_parts",
        (shape((tile_rows, 2 * step, BS), BF16), shape((share, tile_cols, step, BS), F32)),
        slotted + [VMEM],
        [
            pltpu.VMEM((tile_rows, 2 * step, BS), F32),
            pltpu.VMEM((share, tile_cols, 2 * step, BS), BF16),
        ],
    )(*slot_args, gathered)
    with jax.named_scope("users_1_and_2"):
        parts = exchange(message, PLANE)
    message, user_final = call(
        users_sum_kernel,
        "users_sum",
        (shape((tile_rows, step, BS), BF16), shape((step, BS), F32)),
        [VMEM] * 3,
    )(parts, user_zero, user_scale)
    with jax.named_scope("sent_users_1"):
        users = exchange(message, PLANE)
    message = call(
        items_two_kernel,
        "items_2_parts",
        shape((n_row, share, 3, step // 4, BS), BF16),
        slotted + [VMEM] * 3,
        [acc_items],
    )(*slot_args, users, item_sum, user_final)
    with jax.named_scope("items_2"):
        parts = exchange(message.reshape(n_row * share, *message.shape[2:]), ROW + ("x",))
    item_final, user_final = call(
        final_kernel,
        "final",
        (shape((i_dev, emb), BF16), shape((u_dev, emb), BF16)),
        [VMEM, VMEM],
    )(parts.reshape(message.shape), payload)
    return user_final, item_final


def solution(mesh):
    fine = Mesh(mesh.devices.reshape(4, 2, 4, 8, 4), AXES)
    col = PLANE + ("x",)
    in_specs = (
        P(AXES, None),
        P(AXES, None),
        P(AXES),
        P(AXES),
        P(ROW, col, None, None, None),
        P(ROW, col, None),
        P(ROW, col, None),
        P(ROW, col),
    )
    out_specs = (P(AXES, None), P(AXES, None))
    return jax.shard_map(
        per_device, mesh=fine, in_specs=in_specs, out_specs=out_specs, check_vma=False
    )
```
